256 devices in a mesh: section: 32 (over x, z_hi, core), tensor: 8 (over y, z_lo).
Axes of the slice: x: 4, y: 4, z: 8 (z_hi: 4, z_lo: 2; z = z_hi * 2 + z_lo), core: 2. Of those that a mesh axis runs over, the one named last changes fastest.
Arguments:
- act_in: bfloat16 [32, 128, 4096], P('section', None, 'tensor'), may hold values from -6 to 6
- grad_in: bfloat16 [32, 128, 4096], P('section', None, 'tensor'), may hold values from -6 to 6
- held_stash: bfloat16 [32, 2, 128, 4096], P('section', None, None, 'tensor'), may hold values from -6 to 6
- new_batch: bfloat16 [128, 4096], P(None, 'tensor'), may hold values from -6 to 6
- head_grad: bfloat16 [128, 4096], P(None, 'tensor'), may hold values from -6 to 6
- norm_gain: float32 [32, 4096], P('section'), may hold values from 0.1 to 1.9
- w_query: bfloat16 [32, 4096, 4096], P('section', None, 'tensor'), may hold values from -0.09375 to 0.09375
- w_key: bfloat16 [32, 4096, 1024], P('section', None, 'tensor'), may hold values from -0.09375 to 0.09375
- w_value: bfloat16 [32, 4096, 1024], P('section', None, 'tensor'), may hold values from -0.09375 to 0.09375
- w_out: bfloat16 [32, 4096, 4096], P('section', 'tensor'), may hold values from -0.09375 to 0.09375
Outputs:
- act_out: bfloat16 [32, 2, 128, 4096], P('section', None, None, 'tensor')
- grad_out: bfloat16 [32, 2, 128, 4096], P('section', None, None, 'tensor')
The draws below stay inside these ranges and needn't reach their ends.
All inputs are finite; a program needn't handle non-finite values.
Results may differ from the reference program's by a relative error of at most 0.019.
Values may be sent and summed in bfloat16 or wider, within the bound.
A program may use at most 128 MiB of HBM per device.

```python
import jax
import jax.numpy as jnp
from jax import lax

D = 4096
HEADS = 32
KV = 8
HD = 128
TOK = 128
TICKS = 2
N_SECTION = 32
N_TENSOR = 8


def steps_of(own_key, extent, split, low, top_value):
    def one(dim, parts):
        draws = jax.random.uniform(jax.random.fold_in(jax.random.fold_in(own_key, 6), dim), (parts,), jnp.float32, low / len(split), top_value / len(split))
        return jnp.repeat(jnp.exp(draws), extent[dim] // parts).reshape((-1,) + (1,) * (len(extent) - dim - 1))

    gain = one(*split[0])
    for cut in split[1:]:
        gain = gain * one(*cut)
    return gain


def centred(stream_key, extent, deviation, bound, pieces=(), kind=jnp.bfloat16):
    values = deviation * jax.random.normal(stream_key, extent, jnp.float32)
    if pieces:
        values = values * steps_of(stream_key, extent, pieces, -0.22, 0.18)
    return jnp.clip(values, -bound, bound).astype(kind)


def setup_inputs(seed: int = 0) -> dict:
    splits = jax.random.split(jax.random.key(seed), 11)
    act_in = centred(splits[0], (N_SECTION, TOK, D), 1.0, 6.0, ((0, 32), (2, 8)))
    grad_in = centred(splits[1], (N_SECTION, TOK, D), 1.0, 6.0, ((0, 32), (2, 8)))
    held_stash = centred(splits[2], (N_SECTION, TICKS, TOK, D), 1.0, 6.0, ((0, 32), (3, 8)))
    new_batch = centred(splits[3], (TOK, D), 1.0, 6.0, ((1, 8),))
    head_grad = centred(splits[4], (TOK, D), 1.0, 6.0, ((1, 8),))
    norm_gain = jnp.clip(1.0 + 0.18 * jax.random.normal(splits[5], (N_SECTION, D), jnp.float32), 0.1, 1.9)
    w_query = centred(splits[6], (N_SECTION, D, HEADS * HD), D ** -0.5, 0.09375, ((0, 32), (2, 8)))
    w_key = centred(splits[7], (N_SECTION, D, KV * HD), D ** -0.5, 0.09375, ((0, 32), (2, 8)))
    w_value = centred(splits[8], (N_SECTION, D, KV * HD), D ** -0.5, 0.09375, ((0, 32), (2, 8)))
    w_out = centred(splits[9], (N_SECTION, HEADS * HD, D), (HEADS * HD) ** -0.5, 0.09375, ((0, 32), (1, 8)))
    return dict(act_in=act_in, grad_in=grad_in, held_stash=held_stash, new_batch=new_batch, head_grad=head_grad, norm_gain=norm_gain, w_query=w_query, w_key=w_key, w_value=w_value, w_out=w_out)


norm_eps = 1e-05

def attend(query, keys, values):
    n_rows = query.shape[0]
    kv_local = keys.shape[1] // HD
    groups = query.shape[1] // keys.shape[1]
    query_four = query.reshape(n_rows, kv_local, groups, HD)
    keys_three = keys.reshape(n_rows, kv_local, HD)
    values_three = values.reshape(n_rows, kv_local, HD)
    scores = jnp.einsum('tkgd,ukd->kgtu', query_four, keys_three, precision=lax.Precision.HIGHEST) * HD ** (-0.5)
    causal = jnp.arange(n_rows)[:, None] >= jnp.arange(n_rows)[None, :]
    scores = jnp.where(causal, scores, -1e+30)
    peak = lax.optimization_barrier(jnp.max(scores, axis=-1, keepdims=True))
    expo = jnp.exp(scores - peak)
    probs = expo / lax.optimization_barrier(jnp.sum(expo, axis=-1, keepdims=True))
    mixed = jnp.einsum('kgtu,ukd->tkgd', probs, values_three, precision=lax.Precision.HIGHEST)
    return mixed.reshape(n_rows, -1)

def rms_norm(hidden, gain_row):
    x_float = hidden.astype(jnp.float32)
    inv_rms = lax.rsqrt(lax.optimization_barrier(jnp.mean(x_float * x_float, axis=-1, keepdims=True)) + norm_eps)
    normed = (x_float * inv_rms * gain_row.astype(jnp.float32)).astype(jnp.bfloat16)
    return (normed, inv_rms)

def project_in(normed, w_query, w_key, w_value):
    query = jnp.dot(normed, w_query, preferred_element_type=jnp.float32)
    keys = jnp.dot(normed, w_key, preferred_element_type=jnp.float32)
    values = jnp.dot(normed, w_value, preferred_element_type=jnp.float32)
    return (query, keys, values)

def group_partial(normed, w_query, w_key, w_value, w_out):
    query, keys, values = project_in(normed, w_query, w_key, w_value)
    mixed = attend(query, keys, values)
    return jnp.dot(mixed.astype(jnp.bfloat16), w_out, preferred_element_type=jnp.float32)

def group_backward(normed, grad_full, w_query, w_key, w_value, w_out):
    query, keys, values = project_in(normed, w_query, w_key, w_value)
    d_mixed = jnp.dot(grad_full, w_out.T, preferred_element_type=jnp.float32)
    unused, pullback = jax.vjp(attend, query, keys, values)
    d_query, d_keys, d_values = pullback(d_mixed)
    total = jnp.dot(d_query.astype(jnp.bfloat16), w_query.T, preferred_element_type=jnp.float32)
    total = total + jnp.dot(d_keys.astype(jnp.bfloat16), w_key.T, preferred_element_type=jnp.float32)
    return total + jnp.dot(d_values.astype(jnp.bfloat16), w_value.T, preferred_element_type=jnp.float32)

def norm_step(x_float, inv_rms, scaled, row_total, grad_float, full_width):
    result = grad_float + inv_rms * scaled - x_float * (inv_rms * inv_rms * inv_rms) * row_total / full_width
    return result.astype(jnp.bfloat16)

def section_forward(hidden, gain_row, w_query, w_key, w_value, w_out):
    normed, inv_rms = rms_norm(hidden, gain_row)
    q_cols = w_query.shape[1] // N_TENSOR
    k_cols = w_key.shape[1] // N_TENSOR
    attention = jnp.zeros(hidden.shape, jnp.float32)
    for group in range(N_TENSOR):
        partial_value = group_partial(normed, w_query[:, group * q_cols:(group + 1) * q_cols], w_key[:, group * k_cols:(group + 1) * k_cols], w_value[:, group * k_cols:(group + 1) * k_cols], w_out[group * q_cols:(group + 1) * q_cols])
        attention = attention + lax.optimization_barrier(partial_value.astype(jnp.bfloat16)).astype(jnp.float32)
    return (hidden.astype(jnp.float32) + attention).astype(jnp.bfloat16)

def section_backward(hidden, grad_full, gain_row, w_query, w_key, w_value, w_out):
    normed, inv_rms = rms_norm(hidden, gain_row)
    q_cols = w_query.shape[1] // N_TENSOR
    k_cols = w_key.shape[1] // N_TENSOR
    d_norm = jnp.zeros(hidden.shape, jnp.float32)
    for group in range(N_TENSOR):
        part = group_backward(normed, grad_full, w_query[:, group * q_cols:(group + 1) * q_cols], w_key[:, group * k_cols:(group + 1) * k_cols], w_value[:, group * k_cols:(group + 1) * k_cols], w_out[group * q_cols:(group + 1) * q_cols])
        d_norm = d_norm + lax.optimization_barrier(part.astype(jnp.bfloat16)).astype(jnp.float32)
    x_float = hidden.astype(jnp.float32)
    scaled = d_norm * gain_row.astype(jnp.float32)
    row_total = lax.optimization_barrier(jnp.sum(scaled * x_float, axis=-1, keepdims=True))
    return norm_step(x_float, inv_rms, scaled, row_total, grad_full.astype(jnp.float32), hidden.shape[-1])

def reference(act_in, grad_in, held_stash, new_batch, head_grad, norm_gain, w_query, w_key, w_value, w_out):
    layer_inputs = act_in
    forward_list = []
    for tick_num in range(TICKS):
        outputs = lax.map(lambda packed: section_forward(*packed), (layer_inputs, norm_gain, w_query, w_key, w_value, w_out))
        forward_list.append(outputs)
        layer_inputs = jnp.concatenate([new_batch[None], outputs[:-1]], axis=0)
    own_stash = jnp.roll(held_stash, N_SECTION // 2, axis=0)
    grads_now = grad_in
    backward_list = []
    for tick_num in range(TICKS):
        results = lax.map(lambda packed: section_backward(*packed), (own_stash[:, tick_num], grads_now, norm_gain, w_query, w_key, w_value, w_out))
        backward_list.append(results)
        grads_now = jnp.concatenate([results[1:], head_grad[None]], axis=0)
    return (jnp.stack(forward_list, axis=1), jnp.stack(backward_list, axis=1))
```

```python
import functools

import jax
import jax.numpy as jnp
from jax import lax
from jax.experimental import pallas as pl
from jax.experimental.pallas import tpu as pltpu
from jax.sharding import PartitionSpec as P

HD = 128
EPS = 1e-05
MESH = pl.DeviceIdType.MESH
F32 = jnp.float32
BF16 = jnp.bfloat16

REL = [(0, 0), (0, 1), (1, 0), (3, 0), (1, 1), (3, 1), (2, 0), (2, 1)]


def split_bf16(a):
    hi = a.astype(BF16)
    return hi, (a - hi.astype(F32)).astype(BF16)


def mm3(a, b, dims):
    a_hi, a_lo = split_bf16(a)
    b_hi, b_lo = split_bf16(b)

    def dot(u, w):
        return lax.dot_general(u, w, (dims, ((), ())), preferred_element_type=F32)

    return dot(a_hi, b_hi) + (dot(a_hi, b_lo) + dot(a_lo, b_hi))


NN = ((1,), (0,))
NT = ((1,), (1,))


def heads_to_rows(a):
    return jnp.concatenate([a[:, i : i + HD] for i in range(0, a.shape[1], HD)], axis=0)


def rows_to_heads(a, rows):
    return jnp.concatenate([a[i : i + rows] for i in range(0, a.shape[0], rows)], axis=1)


def softmax_probs(query_rows, keys, rows):
    scores = mm3(query_rows, keys, NT) * HD ** (-0.5)
    row = lax.broadcasted_iota(jnp.int32, (rows, rows), 0)
    col = lax.broadcasted_iota(jnp.int32, (rows, rows), 1)
    causal = jnp.concatenate([row >= col] * (scores.shape[0] // rows), axis=0)
    scores = jnp.where(causal, scores, -1e30)
    expo = jnp.exp(scores - jnp.max(scores, axis=-1, keepdims=True))
    return expo / jnp.sum(expo, axis=-1, keepdims=True)


class Gather:
    def __init__(self, buf, recv, sent, dev):
        self.buf, self.recv, self.sent, self.dev = buf, recv, sent, dev

    def copy(self, src, dst, half, to):
        return pltpu.make_async_remote_copy(
            src_ref=self.buf.at[src, half],
            dst_ref=self.buf.at[dst, half],
            send_sem=self.sent,
            recv_sem=self.recv.at[dst, half],
            device_id=self.dev(*to),
            device_id_type=MESH,
        )

    def wait(self, slot, halves=(0, 1)):
        for half in halves:
            self.copy(slot, slot, half, (0, 1)).wait_recv()

    def start(self):
        for half in range(2):
            self.copy(0, 1, half, (0, 1)).start()
            self.copy(0, 3, half, (1, 0)).start()
            self.copy(0, 2, half, (3, 0)).start()

    def relay_first(self):
        for half in range(2):
            self.wait(1, (half,))
            self.copy(1, 5, half, (1, 0)).start()
            self.copy(1, 4, half, (3, 0)).start()
        self.wait(3, (0,))
        self.copy(3, 6, 0, (1, 0)).start()
        self.wait(2, (1,))
        self.copy(2, 6, 1, (3, 0)).start()

    def relay_second(self):
        for half in range(2):
            self.wait(6, (half,))
            self.copy(6, 7, half, (0, 1)).start()

    def wait_near(self):
        self.wait(3, (1,))
        self.wait(2, (0,))

    def wait_far(self):
        for slot in (4, 5, 7):
            self.wait(slot)

    def drain(self):
        rest = self.buf.at[pl.ds(1, 7)]
        pltpu.make_async_copy(rest, rest, self.sent).wait()


class Scatter:
    def __init__(self, parts, out, got, recv, sent, dev):
        self.parts, self.out, self.got = parts, out, got
        self.recv, self.sent, self.dev = recv, sent, dev
        self.half_rows = out.shape[2]

    def copy(self, slot, half, to):
        return pltpu.make_async_remote_copy(
            src_ref=self.out.at[slot, half],
            dst_ref=self.got.at[slot, half],
            send_sem=self.sent,
            recv_sem=self.recv.at[slot, half],
            device_id=self.dev(*to),
            device_id_type=MESH,
        )

    def wait(self, slot, half):
        self.copy(slot, half, (0, 1)).wait_recv()

    def part(self, slot, half):
        return self.parts[slot, pl.ds(half * self.half_rows, self.half_rows), :]

    def push(self, slot, half, to, adds=()):
        total = self.part(slot, half)
        for other in adds:
            total = total + self.got[other, half].astype(F32)
        self.out[slot, half] = total.astype(BF16)
        self.copy(slot, half, to).start()

    def start_far(self):
        for half in range(2):
            self.push(7, half, (0, 1))
            self.push(4, half, (1, 0))
            self.push(5, half, (3, 0))

    def start_near(self):
        self.push(2, 0, (1, 0))
        self.push(3, 1, (3, 0))

    def relay_first(self):
        for half, to in ((0, (3, 0)), (1, (1, 0))):
            self.wait(7, half)
            self.push(6, half, to, (7,))
        for half in range(2):
            self.wait(4, half)
            self.wait(5, half)
            self.push(1, half, (0, 1), (4, 5))

    def relay_second(self):
        self.wait(6, 0)
        self.push(3, 0, (3, 0), (6,))
        self.wait(6, 1)
        self.push(2, 1, (1, 0), (6,))

    def total(self, half):
        for slot in (1, 2, 3):
            self.wait(slot, half)
        total = self.part(0, half)
        for slot in (1, 2, 3):
            total = total + self.got[slot, half].astype(F32)
        return total

    def drain(self):
        rest = self.out.at[pl.ds(1, 7)]
        pltpu.make_async_copy(rest, rest, self.sent).wait()


def kernel(
    act_ref, grad_ref, stash_ref, fresh_ref, head_ref, gain_ref, wq_ref, wk_ref, wv_ref, wo_ref,
    act_out, grad_out,
    w_in, w_out, gains, ag_first, ag_stash, ag_act, ag_grad,
    parts_f, parts_b, outs, gots, acc_f, acc_s, acc_d, sq_f, sq_s, mixed_ref, dqkv_ref,
    moved_act, moved_grad, sent_act, sent_grad, totals, total_out,
    ag_recv, ag_sent, rs_recv, rs_sent, tot_recv, tot_sent, move_send, move_recv, w_sem,
):
    n_section = lax.axis_size("section")
    section = lax.axis_index("section")
    tensor = lax.axis_index("tensor")
    place_y, place_z = tensor // 2, lax.rem(tensor, 2)
    rows, width = act_ref.shape
    half = rows // 2
    q_cols = wq_ref.shape[2]
    k_cols = wk_ref.shape[2]
    full_width = 8 * width

    def owner(dy, dz):
        return lax.rem(place_y + dy, 4) * 2 + lax.rem(place_z + dz, 2)

    def dev(dy, dz):
        return (section, owner(dy, dz))

    def sec(by):
        return (lax.rem(section + by + n_section, n_section), tensor)

    barrier = pltpu.get_barrier_semaphore()
    for dy, dz in REL[1:]:
        pl.semaphore_signal(barrier, inc=1, device_id=dev(dy, dz), device_id_type=MESH)
    for by in (1, -1, n_section // 2):
        pl.semaphore_signal(barrier, inc=1, device_id=sec(by), device_id_type=MESH)

    loads = []
    for slot, (dy, dz) in enumerate(REL):
        who = owner(dy, dz)
        loads += [
            pltpu.make_async_copy(wq_ref.at[who], w_in.at[slot, :, pl.ds(0, q_cols)], w_sem.at[0]),
            pltpu.make_async_copy(wk_ref.at[who], w_in.at[slot, :, pl.ds(q_cols, k_cols)], w_sem.at[0]),
            pltpu.make_async_copy(wv_ref.at[who], w_in.at[slot, :, pl.ds(q_cols + k_cols, k_cols)], w_sem.at[0]),
            pltpu.make_async_copy(
                wo_ref.at[:, pl.ds(pl.multiple_of(who * width, width), width)], w_out.at[slot], w_sem.at[1]
            ),
        ]
    for load in loads:
        load.start()
    ag_first[0, 0] = act_ref[...]
    ag_first[0, 1] = grad_ref[...]
    pl.semaphore_wait(barrier, 10)

    def move(src, dst, index, by):
        return pltpu.make_async_remote_copy(
            src_ref=src,
            dst_ref=dst,
            send_sem=move_send.at[index],
            recv_sem=move_recv.at[index],
            device_id=sec(by),
            device_id_type=MESH,
        )

    recall = move(stash_ref, ag_stash.at[0], 0, n_section // 2)
    recall.start()
    gather = [
        Gather(buf, ag_recv.at[i], ag_sent.at[i], dev)
        for i, buf in enumerate((ag_first, ag_stash, ag_act, ag_grad))
    ]
    first, stash, act_1, grad_1 = gather
    scatter = [
        Scatter(parts, outs.at[i], gots.at[i], rs_recv.at[i], rs_sent.at[i], dev)
        for i, parts in enumerate((parts_f, parts_b, parts_f, parts_b))
    ]
    first.start()

    for slot, (dy, dz) in enumerate(REL):
        gains[slot] = gain_ref[owner(dy, dz)]
    acc_f[...] = jnp.zeros_like(acc_f)
    acc_s[...] = jnp.zeros_like(acc_s)
    acc_d[...] = jnp.zeros_like(acc_d)
    sq_f[...] = jnp.zeros_like(sq_f)
    sq_s[...] = jnp.zeros_like(sq_s)

    def project(block, slot, acc, squares):
        x = block.astype(F32)
        square = x * x
        squares[...] += sum(square[:, i : i + HD] for i in range(0, width, HD))
        scaled = (x * gains[slot]).astype(BF16)
        acc[...] += jnp.dot(scaled, w_in[slot], preferred_element_type=F32)

    def pull_mixed(block, slot):
        acc_d[...] += lax.dot_general(
            block, w_out[slot], (NT, ((), ())), preferred_element_type=F32
        )

    def inverse_rms(squares):
        mean = jnp.sum(squares, axis=-1, keepdims=True) / full_width
        return lax.rsqrt(mean + EPS)

    def forward_attention():
        inv = inverse_rms(sq_f[...])
        qkv = acc_f[...] * inv
        query = heads_to_rows(qkv[:, :q_cols])
        keys = qkv[:, q_cols : q_cols + k_cols]
        values = qkv[:, q_cols + k_cols :]
        probs = softmax_probs(query, keys, rows)
        mixed_ref[...] = rows_to_heads(mm3(probs, values, NN), rows).astype(BF16)

    def forward_parts(lo, hi):
        @pl.loop(lo, hi)
        def _(slot):
            parts_f[slot] = jnp.dot(mixed_ref[...], w_out[slot], preferred_element_type=F32)

    def backward_parts(lo, hi):
        @pl.loop(lo, hi)
        def _(slot):
            parts_b[slot] = lax.dot_general(
                dqkv_ref[...], w_in[slot], (NT, ((), ())), preferred_element_type=F32
            )

    def diagonal():
        row = lax.broadcasted_iota(jnp.int32, (rows, rows), 0)
        col = lax.broadcasted_iota(jnp.int32, (rows, rows), 1)
        return row == col

    def total_copy(tick, slot, mirror, dy, dz):
        return pltpu.make_async_remote_copy(
            src_ref=total_out.at[tick],
            dst_ref=totals.at[tick, mirror],
            send_sem=tot_sent.at[tick],
            recv_sem=tot_recv.at[tick, mirror],
            device_id=dev(dy, dz),
            device_id_type=MESH,
        )

    def backward_attention(tick):
        at = pl.ds(tick * rows, rows)
        raw = acc_s[at, :]
        qkv = raw * inverse_rms(sq_s[at, :])
        query = heads_to_rows(qkv[:, :q_cols])
        keys = qkv[:, q_cols : q_cols + k_cols]
        values = qkv[:, q_cols + k_cols :]
        probs = softmax_probs(query, keys, rows)
        d_mixed = heads_to_rows(acc_d[...])
        d_values = mm3(probs.T, d_mixed, NN)
        d_probs = mm3(d_mixed, values, NT)
        d_scores = probs * (d_probs - jnp.sum(d_probs * probs, axis=-1, keepdims=True))
        d_scores = d_scores * HD ** (-0.5)
        d_query = rows_to_heads(mm3(d_scores, keys, NN), rows)
        d_keys = mm3(d_scores.T, query, NN)
        dqkv = jnp.concatenate([d_query, d_keys, d_values], axis=1).astype(BF16)
        dqkv_ref[...] = dqkv
        share = jnp.sum(dqkv.astype(F32) * raw, axis=-1, keepdims=True)
        line = jnp.sum(jnp.where(diagonal(), share, 0.0), axis=0, keepdims=True)
        total_out[tick] = jnp.broadcast_to(line, total_out.shape[1:])
        for slot, (dy, dz) in enumerate(REL[1:], 1):
            mirror = REL.index(((4 - dy) % 4, dz))
            total_copy(tick, slot, mirror, dy, dz).start()

    def act_finish(tick, own, rs):
        for i in range(2):
            at = pl.ds(i * half, half)
            out = (own(i).astype(F32) + rs.total(i)).astype(BF16)
            act_out[tick, at, :] = out
            if tick == 0:
                sent_act[at, :] = out

    def grad_finish(tick, own, rs):
        for slot in range(1, 8):
            total_copy(tick, slot, slot, 0, 1).wait_recv()
        line = total_out[tick]
        for slot in range(1, 8):
            line = line + totals[tick, slot]
        full = jnp.where(diagonal(), line[0:1, :], 0.0)
        row_total = jnp.sum(full, axis=-1, keepdims=True)
        inv = inverse_rms(sq_s[pl.ds(tick * rows, rows), :])
        for i in range(2):
            at = pl.ds(i * half, half)
            cut = slice(i * half, (i + 1) * half)
            x = ag_stash[0, tick, at, :].astype(F32)
            scaled = rs.total(i) * gains[0]
            inv_i = inv[cut]
            out = (
                own(i).astype(F32)
                + inv_i * scaled
                - x * (inv_i * inv_i * inv_i) * row_total[cut] / full_width
            ).astype(BF16)
            grad_out[tick, at, :] = out
            if tick == 0:
                sent_grad[at, :] = out

    first.relay_first()
    recall.wait_recv()
    stash.start()
    whole_in, whole_out = w_in.at[...], w_out.at[...]
    pltpu.make_async_copy(whole_in, whole_in, w_sem.at[0]).wait()
    pltpu.make_async_copy(whole_out, whole_out, w_sem.at[1]).wait()
    first.wait_near()

    def first_chunks(lo, hi):
        @pl.loop(lo, hi)
        def _(slot):
            project(ag_first[slot, 0], slot, acc_f, sq_f)
            pull_mixed(ag_first[slot, 1], slot)

    first_chunks(0, 4)
    first.relay_second()
    first.wait_far()
    first_chunks(4, 8)
    forward_attention()
    forward_parts(4, 8)
    scatter[0].start_far()
    forward_parts(0, 4)
    scatter[0].start_near()
    stash.relay_first()
    scatter[0].relay_first()
    stash.wait_near()

    def stash_chunks(lo, hi):
        @pl.loop(lo, hi)
        def _(slot):
            project(ag_stash[slot].reshape(2 * rows, width), slot, acc_s, sq_s)

    stash_chunks(0, 4)
    stash.relay_second()
    scatter[0].relay_second()
    act_finish(0, lambda i: ag_first[0, 0, pl.ds(i * half, half), :], scatter[0])
    shift_act = move(sent_act, moved_act, 1, 1)
    shift_act.start()
    stash.wait_far()
    stash_chunks(4, 8)
    backward_attention(0)
    backward_parts(4, 8)
    scatter[1].start_far()
    backward_parts(0, 4)
    scatter[1].start_near()

    shift_act.wait_recv()
    for i in range(2):
        at = pl.ds(i * half, half)
        ag_act[0, i] = jnp.where(section == 0, fresh_ref[at, :], moved_act[at, :])
    act_1.start()
    scatter[1].relay_first()
    acc_f[...] = jnp.zeros_like(acc_f)
    acc_d[...] = jnp.zeros_like(acc_d)
    sq_f[...] = jnp.zeros_like(sq_f)
    act_1.relay_first()
    scatter[1].relay_second()
    act_1.relay_second()
    grad_finish(0, lambda i: ag_first[0, 1, pl.ds(i * half, half), :], scatter[1])
    shift_grad = move(sent_grad, moved_grad, 2, -1)
    shift_grad.start()
    act_1.wait_near()
    act_1.wait_far()

    @pl.loop(0, 8)
    def _(slot):
        project(ag_act[slot].reshape(rows, width), slot, acc_f, sq_f)

    forward_attention()
    forward_parts(4, 8)
    scatter[2].start_far()
    forward_parts(0, 4)
    scatter[2].start_near()

    shift_grad.wait_recv()
    for i in range(2):
        at = pl.ds(i * half, half)
        ag_grad[0, i] = jnp.where(section == n_section - 1, head_ref[at, :], moved_grad[at, :])
    grad_1.start()
    scatter[2].relay_first()
    grad_1.relay_first()
    scatter[2].relay_second()
    grad_1.relay_second()
    act_finish(1, lambda i: ag_act[0, i], scatter[2])
    grad_1.wait_near()
    grad_1.wait_far()

    @pl.loop(0, 8)
    def _(slot):
        pull_mixed(ag_grad[slot].reshape(rows, width), slot)

    backward_attention(1)
    backward_parts(4, 8)
    scatter[3].start_far()
    backward_parts(0, 4)
    scatter[3].start_near()
    scatter[3].relay_first()
    scatter[3].relay_second()
    grad_finish(1, lambda i: ag_grad[0, i], scatter[3])

    for one in gather + scatter:
        one.drain()
    for tick in range(2):
        rest = totals.at[tick, pl.ds(1, 7)]
        pltpu.make_async_copy(rest, rest, tot_sent.at[tick]).wait()
    for one in (recall, shift_act, shift_grad):
        one.wait_send()


def per_device(
    act_in, grad_in, held_stash, new_batch, head_grad, norm_gain, w_query, w_key, w_value, w_out
):
    rows, width = act_in.shape[1:]
    half = rows // 2
    q_cols, k_cols = w_query.shape[2], w_key.shape[2]
    cols = q_cols + 2 * k_cols
    vmem = pl.BlockSpec(memory_space=pltpu.VMEM)
    hbm = pl.BlockSpec(memory_space=pl.ANY)
    out = jax.ShapeDtypeStruct((2, rows, width), BF16)
    scratch = [
        pltpu.VMEM((8, width, cols), BF16),
        pltpu.VMEM((8, q_cols, width), BF16),
        pltpu.VMEM((8, 1, width), F32),
        pltpu.VMEM((8, 2, rows, width), BF16),
        pltpu.VMEM((8, 2, rows, width), BF16),
        pltpu.VMEM((8, 2, half, width), BF16),
        pltpu.VMEM((8, 2, half, width), BF16),
        pltpu.VMEM((8, rows, width), F32),
        pltpu.VMEM((8, rows, width), F32),
        pltpu.VMEM((4, 8, 2, half, width), BF16),
        pltpu.VMEM((4, 8, 2, half, width), BF16),
        pltpu.VMEM((rows, cols), F32),
        pltpu.VMEM((2 * rows, cols), F32),
        pltpu.VMEM((rows, q_cols), F32),
        pltpu.VMEM((rows, HD), F32),
        pltpu.VMEM((2 * rows, HD), F32),
        pltpu.VMEM((rows, q_cols), BF16),
        pltpu.VMEM((rows, cols), BF16),
        pltpu.VMEM((rows, width), BF16),
        pltpu.VMEM((rows, width), BF16),
        pltpu.VMEM((rows, width), BF16),
        pltpu.VMEM((rows, width), BF16),
        pltpu.VMEM((2, 8, 8, rows), F32),
        pltpu.VMEM((2, 8, rows), F32),
        pltpu.SemaphoreType.DMA((4, 8, 2)),
        pltpu.SemaphoreType.DMA((4,)),
        pltpu.SemaphoreType.DMA((4, 8, 2)),
        pltpu.SemaphoreType.DMA((4,)),
        pltpu.SemaphoreType.DMA((2, 8)),
        pltpu.SemaphoreType.DMA((2,)),
        pltpu.SemaphoreType.DMA((3,)),
        pltpu.SemaphoreType.DMA((3,)),
        pltpu.SemaphoreType.DMA((2,)),
    ]
    acts, grads = pl.pallas_call(
        kernel,
        out_shape=(out, out),
        in_specs=[vmem] * 6 + [hbm] * 4,
        out_specs=(vmem, vmem),
        scratch_shapes=scratch,
        compiler_params=pltpu.CompilerParams(
            collective_id=0, has_side_effects=True, vmem_limit_bytes=52 << 20
        ),
    )(
        act_in[0],
        grad_in[0],
        held_stash[0],
        new_batch,
        head_grad,
        norm_gain.reshape(8, 1, width),
        w_query.reshape(8, width, q_cols),
        w_key.reshape(8, width, k_cols),
        w_value.reshape(8, width, k_cols),
        w_out[0],
    )
    return acts[None], grads[None]


def solution(mesh):
    in_specs = (
        P("section", None, "tensor"),
        P("section", None, "tensor"),
        P("section", None, None, "tensor"),
        P(None, "tensor"),
        P(None, "tensor"),
        P("section", None),
        P("section", None, "tensor"),
        P("section", None, "tensor"),
        P("section", None, "tensor"),
        P("section", "tensor", None),
    )
    out_specs = (P("section", None, None, "tensor"), P("section", None, None, "tensor"))
    return jax.shard_map(
        per_device, mesh=mesh, in_specs=in_specs, out_specs=out_specs, check_vma=False
    )
```

```python
import functools

import jax
import jax.numpy as jnp
from jax import lax
from jax.experimental import pallas as pl
from jax.experimental.pallas import tpu as pltpu
from jax.sharding import PartitionSpec as P

HD = 128
EPS = 1e-05
MESH = pl.DeviceIdType.MESH
F32 = jnp.float32
BF16 = jnp.bfloat16

REL = [(0, 0), (0, 1), (1, 0), (3, 0), (1, 1), (3, 1), (2, 0), (2, 1)]


def split_bf16(a):
    hi = a.astype(BF16)
    return hi, (a - hi.astype(F32)).astype(BF16)


def mm3(a, b, dims):
    a_hi, a_lo = split_bf16(a)
    b_hi, b_lo = split_bf16(b)

    def dot(u, w):
        return lax.dot_general(u, w, (dims, ((), ())), preferred_element_type=F32)

    return dot(a_hi, b_hi) + (dot(a_hi, b_lo) + dot(a_lo, b_hi))


NN = ((1,), (0,))
NT = ((1,), (1,))


def heads_to_rows(a):
    return jnp.concatenate([a[:, i : i + HD] for i in range(0, a.shape[1], HD)], axis=0)


def rows_to_heads(a, rows):
    return jnp.concatenate([a[i : i + rows] for i in range(0, a.shape[0], rows)], axis=1)


def softmax_probs(query_rows, keys, rows):
    scores = mm3(query_rows, keys, NT) * HD ** (-0.5)
    row = lax.broadcasted_iota(jnp.int32, (rows, rows), 0)
    col = lax.broadcasted_iota(jnp.int32, (rows, rows), 1)
    causal = jnp.concatenate([row >= col] * (scores.shape[0] // rows), axis=0)
    scores = jnp.where(causal, scores, -1e30)
    expo = jnp.exp(scores - jnp.max(scores, axis=-1, keepdims=True))
    return expo / jnp.sum(expo, axis=-1, keepdims=True)


class Gather:
    def __init__(self, buf, recv, sent, dev, source, flip):
        self.buf, self.recv, self.sent, self.dev = buf, recv, sent, dev
        self.source, self.flip = source, flip
        self.here = set()

    def copy(self, src, dst, half, to):
        return pltpu.make_async_remote_copy(
            src_ref=self.buf.at[src, half],
            dst_ref=self.buf.at[dst, half],
            send_sem=self.sent,
            recv_sem=self.recv.at[dst, half],
            device_id=self.dev(*to),
            device_id_type=MESH,
        )

    def ready(self, slot, halves=(0, 1)):
        for half in halves:
            if slot and (slot, half) not in self.here:
                self.here.add((slot, half))
                self.copy(slot, slot, half, (0, 1)).wait_recv()

    def start(self, half):
        self.source(self, half)
        self.copy(0, 1, half, (0, 1)).start()
        self.copy(0, 3, half, (1, 0)).start()
        self.copy(0, 2, 1 - half if self.flip else half, (3, 0)).start()

    def across(self, half):
        self.ready(1, (half,))
        self.copy(1, 5, half, (1, 0)).start()
        self.copy(1, 4, half, (3, 0)).start()

    def along_up(self):
        self.ready(3, (0,))
        self.copy(3, 6, 0, (1, 0)).start()

    def along_down(self):
        self.ready(2, (1,))
        self.copy(2, 6, 1, (3, 0)).start()

    def last(self, half):
        self.ready(6, (half,))
        self.copy(6, 7, half, (0, 1)).start()

    def drain(self):
        rest = self.buf.at[pl.ds(1, 7)]
        pltpu.make_async_copy(rest, rest, self.sent).wait()


class Scatter:
    def __init__(self, parts, out, got, recv, sent, dev):
        self.parts, self.out, self.got = parts, out, got
        self.recv, self.sent, self.dev = recv, sent, dev
        self.half_rows = out.shape[2]

    def copy(self, slot, half, to):
        return pltpu.make_async_remote_copy(
            src_ref=self.out.at[slot, half],
            dst_ref=self.got.at[slot, half],
            send_sem=self.sent,
            recv_sem=self.recv.at[slot, half],
            device_id=self.dev(*to),
            device_id_type=MESH,
        )

    def wait(self, slot, half):
        self.copy(slot, half, (0, 1)).wait_recv()

    def part(self, slot, half):
        return self.parts[slot, pl.ds(half * self.half_rows, self.half_rows), :]

    def push(self, slot, half, to, adds=()):
        total = self.part(slot, half)
        for other in adds:
            total = total + self.got[other, half].astype(F32)
        self.out[slot, half] = total.astype(BF16)
        self.copy(slot, half, to).start()

    def begin(self, slot):
        to = {7: (0, 1), 4: (1, 0), 5: (3, 0), 2: (1, 0), 3: (3, 0)}[slot]
        for half in {2: (0,), 3: (1,)}.get(slot, (0, 1)):
            self.push(slot, half, to)

    def last(self, half):
        self.wait(7, half)
        self.push(6, half, (1, 0) if half else (3, 0), (7,))

    def across(self, half):
        self.wait(4, half)
        self.wait(5, half)
        self.push(1, half, (0, 1), (4, 5))

    def along_down(self):
        self.wait(6, 0)
        self.push(3, 0, (3, 0), (6,))

    def along_up(self):
        self.wait(6, 1)
        self.push(2, 1, (1, 0), (6,))

    def total(self, half):
        for slot in (1, 2, 3):
            self.wait(slot, half)
        total = self.part(0, half)
        for slot in (1, 2, 3):
            total = total + self.got[slot, half].astype(F32)
        return total

    def drain(self):
        rest = self.out.at[pl.ds(1, 7)]
        pltpu.make_async_copy(rest, rest, self.sent).wait()


def kernel(
    act_ref, grad_ref, stash_ref, fresh_ref, head_ref, gain_ref, wq_ref, wk_ref, wv_ref, wo_ref,
    act_out, grad_out,
    w_in, w_out, gains, edges, ag, parts_f, parts_b, outs, gots, acc_f, acc_s, acc_d, sq_f, sq_s,
    mixed_ref, dqkv_ref, moved, shifted, totals, total_out,
    ag_recv, ag_sent, rs_recv, rs_sent, tot_recv, tot_sent, recall_send, recall_recv,
    move_send, move_recv, load_sem, w_sem,
):
    n_section = lax.axis_size("section")
    section = lax.axis_index("section")
    tensor = lax.axis_index("tensor")
    place_y, place_z = tensor // 2, lax.rem(tensor, 2)
    half, width = act_ref.shape[1:]
    rows = 2 * half
    q_cols = wq_ref.shape[2]
    k_cols = wk_ref.shape[2]
    full_width = 8 * width

    def owner(dy, dz):
        return lax.rem(place_y + dy, 4) * 2 + lax.rem(place_z + dz, 2)

    def dev(dy, dz):
        return (section, owner(dy, dz))

    def sec(by):
        return (lax.rem(section + by + n_section, n_section), tensor)

    barrier = pltpu.get_barrier_semaphore()
    for dy, dz in REL[1:]:
        pl.semaphore_signal(barrier, inc=1, device_id=dev(dy, dz), device_id_type=MESH)
    for by in (1, -1, n_section // 2):
        pl.semaphore_signal(barrier, inc=1, device_id=sec(by), device_id_type=MESH)

    def own(one, half):
        pass

    def recalled(tick):
        def source(one, half):
            if half == 0:
                recalls[tick].wait_recv()

        return source

    def arrived(index, at_edge):
        def source(one, part):
            shift(index, part, 1).wait_recv()
            edge = edges[index, pl.ds(part * half, half), :]
            one.buf[0, part] = jnp.where(at_edge, edge, moved[index, part])

        return source

    sources = (
        own, own, recalled(0), recalled(1),
        arrived(0, section == 0), arrived(1, section == n_section - 1),
    )
    a0, g0, s0, s1, a1, g1 = [
        Gather(ag.at[i], ag_recv.at[i], ag_sent.at[i], dev, source, i < 4)
        for i, source in enumerate(sources)
    ]
    rs_a0, rs_g0, rs_a1, rs_g1 = [
        Scatter(parts, outs.at[i], gots.at[i], rs_recv.at[i], rs_sent.at[i], dev)
        for i, parts in enumerate((parts_f, parts_b, parts_f, parts_b))
    ]

    loads = [
        pltpu.make_async_copy(act_ref, a0.buf.at[0], load_sem.at[0]),
        pltpu.make_async_copy(grad_ref, g0.buf.at[0], load_sem.at[1]),
    ]
    for slot, (dy, dz) in enumerate(REL):
        loads.append(pltpu.make_async_copy(gain_ref.at[owner(dy, dz)], gains.at[slot], load_sem.at[2]))
    for slot, (dy, dz) in enumerate(REL):
        who = owner(dy, dz)
        loads += [
            pltpu.make_async_copy(wq_ref.at[who], w_in.at[slot, :, pl.ds(0, q_cols)], w_sem.at[0]),
            pltpu.make_async_copy(wk_ref.at[who], w_in.at[slot, :, pl.ds(q_cols, k_cols)], w_sem.at[0]),
            pltpu.make_async_copy(wv_ref.at[who], w_in.at[slot, :, pl.ds(q_cols + k_cols, k_cols)], w_sem.at[0]),
        ]
    for slot, (dy, dz) in enumerate(REL):
        at = pl.ds(pl.multiple_of(owner(dy, dz) * width, width), width)
        loads.append(pltpu.make_async_copy(wo_ref.at[:, at], w_out.at[slot], w_sem.at[1]))
    loads += [
        pltpu.make_async_copy(fresh_ref, edges.at[0], load_sem.at[3]),
        pltpu.make_async_copy(head_ref, edges.at[1], load_sem.at[4]),
    ]
    for load in loads[:10]:
        load.start()
    loads[0].wait()
    loads[1].wait()
    pl.semaphore_wait(barrier, 10)

    recalls = [
        pltpu.make_async_remote_copy(
            src_ref=stash_ref.at[tick],
            dst_ref=one.buf.at[0],
            send_sem=recall_send.at[tick],
            recv_sem=recall_recv.at[tick],
            device_id=sec(n_section // 2),
            device_id_type=MESH,
        )
        for tick, one in enumerate((s0, s1))
    ]

    def shift(index, part, by):
        return pltpu.make_async_remote_copy(
            src_ref=shifted.at[index, part],
            dst_ref=moved.at[index, part],
            send_sem=move_send.at[index, part],
            recv_sem=move_recv.at[index, part],
            device_id=sec(by),
            device_id_type=MESH,
        )

    def clear(*refs):
        for ref in refs:
            ref[...] = jnp.zeros_like(ref)

    def whole(buf, slot):
        return buf[slot].reshape(rows, width)

    def project(one, acc, squares, lo, hi):
        for slot in range(lo, hi):
            one.ready(slot)

        @pl.loop(lo, hi)
        def _(slot):
            x = whole(one.buf, slot).astype(F32)
            square = x * x
            squares[...] += sum(square[:, i : i + HD] for i in range(0, width, HD))
            scaled = (x * gains[slot]).astype(BF16)
            acc[...] += jnp.dot(scaled, w_in[slot], preferred_element_type=F32)

    def pull_mixed(one, lo, hi):
        for slot in range(lo, hi):
            one.ready(slot)

        @pl.loop(lo, hi)
        def _(slot):
            acc_d[...] += lax.dot_general(
                whole(one.buf, slot), w_out[slot], (NT, ((), ())), preferred_element_type=F32
            )

    def inverse_rms(squares):
        mean = jnp.sum(squares, axis=-1, keepdims=True) / full_width
        return lax.rsqrt(mean + EPS)

    def forward_attention():
        qkv = acc_f[...] * inverse_rms(sq_f[...])
        query = heads_to_rows(qkv[:, :q_cols])
        keys = qkv[:, q_cols : q_cols + k_cols]
        values = qkv[:, q_cols + k_cols :]
        probs = softmax_probs(query, keys, rows)
        mixed_ref[...] = rows_to_heads(mm3(probs, values, NN), rows).astype(BF16)

    def forward_parts(lo, hi):
        @pl.loop(lo, hi)
        def _(slot):
            parts_f[slot] = jnp.dot(mixed_ref[...], w_out[slot], preferred_element_type=F32)

    def backward_parts(lo, hi):
        @pl.loop(lo, hi)
        def _(slot):
            parts_b[slot] = lax.dot_general(
                dqkv_ref[...], w_in[slot], (NT, ((), ())), preferred_element_type=F32
            )

    def diagonal():
        row = lax.broadcasted_iota(jnp.int32, (rows, rows), 0)
        col = lax.broadcasted_iota(jnp.int32, (rows, rows), 1)
        return row == col

    def total_copy(tick, mirror, dy, dz):
        return pltpu.make_async_remote_copy(
            src_ref=total_out.at[tick],
            dst_ref=totals.at[tick, mirror],
            send_sem=tot_sent.at[tick],
            recv_sem=tot_recv.at[tick, mirror],
            device_id=dev(dy, dz),
            device_id_type=MESH,
        )

    def backward_attention(tick):
        raw = acc_s[tick]
        qkv = raw * inverse_rms(sq_s[tick])
        query = heads_to_rows(qkv[:, :q_cols])
        keys = qkv[:, q_cols : q_cols + k_cols]
        values = qkv[:, q_cols + k_cols :]
        probs = softmax_probs(query, keys, rows)
        d_mixed = heads_to_rows(acc_d[...])
        d_values = mm3(probs.T, d_mixed, NN)
        d_probs = mm3(d_mixed, values, NT)
        d_scores = probs * (d_probs - jnp.sum(d_probs * probs, axis=-1, keepdims=True))
        d_scores = d_scores * HD ** (-0.5)
        d_query = rows_to_heads(mm3(d_scores, keys, NN), rows)
        d_keys = mm3(d_scores.T, query, NN)
        dqkv = jnp.concatenate([d_query, d_keys, d_values], axis=1).astype(BF16)
        dqkv_ref[...] = dqkv
        share = jnp.sum(dqkv.astype(F32) * raw, axis=-1, keepdims=True)
        line = jnp.sum(jnp.where(diagonal(), share, 0.0), axis=0, keepdims=True)
        total_out[tick] = jnp.broadcast_to(line, total_out.shape[1:])

    def send_totals(tick):
        for dy, dz in REL[1:]:
            total_copy(tick, REL.index(((4 - dy) % 4, dz)), dy, dz).start()

    def act_finish(tick, one, rs, i):
        out = (one.buf[0, i].astype(F32) + rs.total(i)).astype(BF16)
        act_out[tick, pl.ds(i * half, half), :] = out
        if tick == 0:
            shifted[0, i] = out
            shift(0, i, 1).start()

    def grad_finish(tick, one, stashed, rs, i):
        if i == 0:
            for slot in range(1, 8):
                total_copy(tick, slot, 0, 1).wait_recv()
        line = total_out[tick]
        for slot in range(1, 8):
            line = line + totals[tick, slot]
        full = jnp.where(diagonal(), line[0:1, :], 0.0)
        cut = slice(i * half, (i + 1) * half)
        row_total = jnp.sum(full[cut], axis=-1, keepdims=True)
        inv = inverse_rms(sq_s[tick, pl.ds(i * half, half), :])
        x = stashed.buf[0, i].astype(F32)
        scaled = rs.total(i) * gains[0]
        out = (
            one.buf[0, i].astype(F32)
            + inv * scaled
            - x * (inv * inv * inv) * row_total / full_width
        ).astype(BF16)
        grad_out[tick, pl.ds(i * half, half), :] = out
        if tick == 0:
            shifted[1, i] = out
            shift(1, i, -1).start()

    def start_loads():
        for load in loads[10:]:
            load.start()
        recalls[0].start()
        recalls[1].start()

    def wait_weights():
        for buf, sem in ((gains, load_sem.at[2]), (w_in, w_sem.at[0]), (w_out, w_sem.at[1])):
            pltpu.make_async_copy(buf, buf, sem).wait()
        loads[-2].wait()
        loads[-1].wait()

    a0.start(0)
    a0.start(1)
    start_loads()
    clear(acc_f, acc_s, acc_d, sq_f, sq_s)
    g0.start(0)
    g0.start(1)
    a0.along_down()
    a0.along_up()
    wait_weights()
    a0.across(0)
    a0.across(1)
    g0.along_down()
    s0.start(0)
    g0.along_up()
    pull_mixed(g0, 0, 1)
    a0.last(0)
    g0.across(0)
    a0.last(1)
    project(a0, acc_f, sq_f, 0, 1)
    project(a0, acc_f, sq_f, 3, 4)
    s0.start(1)
    s0.along_up()
    g0.last(1)
    pull_mixed(g0, 3, 4)
    project(a0, acc_f, sq_f, 6, 7)
    pull_mixed(g0, 1, 2)
    project(a0, acc_f, sq_f, 4, 5)
    s0.along_down()
    g0.last(0)
    project(a0, acc_f, sq_f, 5, 6)
    project(a0, acc_f, sq_f, 7, 8)
    s0.across(0)
    project(a0, acc_f, sq_f, 1, 3)
    project(s0, acc_s.at[0], sq_s.at[0], 0, 1)
    forward_attention()
    clear(acc_f, sq_f)
    forward_parts(6, 8)
    rs_a0.begin(7)
    project(s0, acc_s.at[0], sq_s.at[0], 1, 2)
    g0.across(1)
    s0.last(1)
    forward_parts(5, 6)
    s0.across(1)
    s0.last(0)
    forward_parts(4, 5)
    rs_a0.begin(4)
    pull_mixed(g0, 2, 3)
    forward_parts(0, 2)
    rs_a0.begin(5)
    rs_a0.last(1)
    pull_mixed(g0, 4, 6)
    s1.start(0)
    rs_a0.last(0)
    s1.start(1)
    forward_parts(2, 4)
    rs_a0.begin(2)
    pull_mixed(g0, 6, 7)
    project(s0, acc_s.at[0], sq_s.at[0], 2, 4)
    rs_a0.across(0)
    project(s0, acc_s.at[0], sq_s.at[0], 4, 5)
    rs_a0.begin(3)
    pull_mixed(g0, 7, 8)
    project(s1, acc_s.at[1], sq_s.at[1], 0, 1)
    project(s0, acc_s.at[0], sq_s.at[0], 7, 8)
    project(s0, acc_s.at[0], sq_s.at[0], 5, 7)
    backward_attention(0)
    backward_parts(7, 8)
    rs_g0.begin(7)
    rs_a0.along_up()
    clear(acc_d)
    rs_a0.along_down()
    backward_parts(4, 5)
    rs_g0.begin(4)
    backward_parts(5, 6)
    rs_g0.begin(5)
    rs_a0.across(1)
    backward_parts(6, 7)
    project(s1, acc_s.at[1], sq_s.at[1], 2, 3)
    rs_g0.last(0)
    rs_g0.last(1)
    act_finish(0, a0, rs_a0, 0)
    act_finish(0, a0, rs_a0, 1)
    s1.across(0)
    backward_parts(1, 2)
    rs_g0.across(0)
    backward_parts(2, 3)
    rs_g0.begin(2)
    backward_parts(0, 1)
    send_totals(0)
    backward_parts(3, 4)
    rs_g0.across(1)
    rs_g0.begin(3)
    rs_g0.along_down()
    rs_g0.along_up()
    a1.start(0)
    a1.start(1)
    grad_finish(0, g0, s0, rs_g0, 0)
    grad_finish(0, g0, s0, rs_g0, 1)
    a1.across(0)
    a1.across(1)
    a1.along_down()
    a1.along_up()
    g1.start(0)
    s1.along_up()
    project(a1, acc_f, sq_f, 0, 1)
    project(a1, acc_f, sq_f, 2, 3)
    g1.start(1)
    pull_mixed(g1, 0, 1)
    project(a1, acc_f, sq_f, 5, 6)
    s1.along_down()
    a1.last(0)
    a1.last(1)
    project(s1, acc_s.at[1], sq_s.at[1], 1, 2)
    project(a1, acc_f, sq_f, 4, 5)
    g1.along_up()
    s1.across(1)
    project(a1, acc_f, sq_f, 6, 7)
    s1.last(0)
    g1.along_down()
    g1.across(0)
    g1.across(1)
    project(a1, acc_f, sq_f, 3, 4)
    s1.last(1)
    pull_mixed(g1, 1, 2)
    pull_mixed(g1, 3, 4)
    project(s1, acc_s.at[1], sq_s.at[1], 3, 4)
    project(a1, acc_f, sq_f, 7, 8)
    g1.last(0)
    project(a1, acc_f, sq_f, 1, 2)
    forward_attention()
    forward_parts(6, 7)
    g1.last(1)
    forward_parts(2, 3)
    rs_a1.begin(2)
    forward_parts(7, 8)
    rs_a1.begin(7)
    project(s1, acc_s.at[1], sq_s.at[1], 4, 5)
    forward_parts(3, 4)
    rs_a1.begin(3)
    project(s1, acc_s.at[1], sq_s.at[1], 5, 6)
    forward_parts(5, 6)
    rs_a1.begin(5)
    project(s1, acc_s.at[1], sq_s.at[1], 7, 8)
    pull_mixed(g1, 6, 7)
    forward_parts(4, 5)
    rs_a1.begin(4)
    project(s1, acc_s.at[1], sq_s.at[1], 6, 7)
    pull_mixed(g1, 2, 3)
    pull_mixed(g1, 4, 6)
    pull_mixed(g1, 7, 8)
    backward_attention(1)
    backward_parts(7, 8)
    rs_g1.begin(7)
    backward_parts(5, 6)
    rs_g1.begin(5)
    forward_parts(0, 1)
    rs_a1.last(1)
    forward_parts(1, 2)
    rs_a1.last(0)
    backward_parts(1, 2)
    backward_parts(4, 5)
    send_totals(1)
    rs_g1.begin(4)
    rs_a1.across(1)
    rs_a1.across(0)
    backward_parts(6, 7)
    rs_g1.last(0)
    rs_g1.last(1)
    backward_parts(0, 1)
    backward_parts(3, 4)
    rs_g1.begin(3)
    rs_a1.along_up()
    rs_g1.across(1)
    rs_g1.across(0)
    backward_parts(2, 3)
    rs_g1.begin(2)
    rs_a1.along_down()
    rs_g1.along_down()
    rs_g1.along_up()
    act_finish(1, a1, rs_a1, 0)
    act_finish(1, a1, rs_a1, 1)
    grad_finish(1, g1, s1, rs_g1, 0)
    grad_finish(1, g1, s1, rs_g1, 1)

    for one in (a0, g0, s0, s1, a1, g1, rs_a0, rs_g0, rs_a1, rs_g1):
        one.drain()
    for tick in range(2):
        rest = totals.at[tick, pl.ds(1, 7)]
        pltpu.make_async_copy(rest, rest, tot_sent.at[tick]).wait()
    for one in recalls:
        one.wait_send()
    for i in range(2):
        shift(0, i, 1).wait_send()
        shift(1, i, -1).wait_send()


def per_device(
    act_in, grad_in, held_stash, new_batch, head_grad, norm_gain, w_query, w_key, w_value, w_out
):
    rows, width = act_in.shape[1:]
    half = rows // 2
    q_cols, k_cols = w_query.shape[2], w_key.shape[2]
    cols = q_cols + 2 * k_cols
    vmem = pl.BlockSpec(memory_space=pltpu.VMEM)
    hbm = pl.BlockSpec(memory_space=pl.ANY)
    out = jax.ShapeDtypeStruct((2, rows, width), BF16)
    scratch = [
        pltpu.VMEM((8, width, cols), BF16),
        pltpu.VMEM((8, q_cols, width), BF16),
        pltpu.VMEM((8, 1, width), F32),
        pltpu.VMEM((2, rows, width), BF16),
        pltpu.VMEM((6, 8, 2, half, width), BF16),
        pltpu.VMEM((8, rows, width), F32),
        pltpu.VMEM((8, rows, width), F32),
        pltpu.VMEM((4, 8, 2, half, width), BF16),
        pltpu.VMEM((4, 8, 2, half, width), BF16),
        pltpu.VMEM((rows, cols), F32),
        pltpu.VMEM((2, rows, cols), F32),
        pltpu.VMEM((rows, q_cols), F32),
        pltpu.VMEM((rows, HD), F32),
        pltpu.VMEM((2, rows, HD), F32),
        pltpu.VMEM((rows, q_cols), BF16),
        pltpu.VMEM((rows, cols), BF16),
        pltpu.VMEM((2, 2, half, width), BF16),
        pltpu.VMEM((2, 2, half, width), BF16),
        pltpu.VMEM((2, 8, 8, rows), F32),
        pltpu.VMEM((2, 8, rows), F32),
        pltpu.SemaphoreType.DMA((6, 8, 2)),
        pltpu.SemaphoreType.DMA((6,)),
        pltpu.SemaphoreType.DMA((4, 8, 2)),
        pltpu.SemaphoreType.DMA((4,)),
        pltpu.SemaphoreType.DMA((2, 8)),
        pltpu.SemaphoreType.DMA((2,)),
        pltpu.SemaphoreType.DMA((2,)),
        pltpu.SemaphoreType.DMA((2,)),
        pltpu.SemaphoreType.DMA((2, 2)),
        pltpu.SemaphoreType.DMA((2, 2)),
        pltpu.SemaphoreType.DMA((5,)),
        pltpu.SemaphoreType.DMA((2,)),
    ]
    acts, grads = pl.pallas_call(
        kernel,
        out_shape=(out, out),
        in_specs=[hbm] * 10,
        out_specs=(vmem, vmem),
        scratch_shapes=scratch,
        compiler_params=pltpu.CompilerParams(
            collective_id=0, has_side_effects=True, vmem_limit_bytes=60 << 20
        ),
    )(
        act_in.reshape(2, half, width),
        grad_in.reshape(2, half, width),
        held_stash.reshape(2, 2, half, width),
        new_batch,
        head_grad,
        norm_gain.reshape(8, 1, width),
        w_query.reshape(8, width, q_cols),
        w_key.reshape(8, width, k_cols),
        w_value.reshape(8, width, k_cols),
        w_out[0],
    )
    return acts[None], grads[None]


def solution(mesh):
    in_specs = (
        P("section", None, "tensor"),
        P("section", None, "tensor"),
        P("section", None, None, "tensor"),
        P(None, "tensor"),
        P(None, "tensor"),
        P("section", None),
        P("section", None, "tensor"),
        P("section", None, "tensor"),
        P("section", None, "tensor"),
        P("section", "tensor", None),
    )
    out_specs = (P("section", None, None, "tensor"), P("section", None, None, "tensor"))
    return jax.shard_map(
        per_device, mesh=mesh, in_specs=in_specs, out_specs=out_specs, check_vma=False
    )
```

```python
import functools

import jax
import jax.numpy as jnp
from jax import lax
from jax.experimental import pallas as pl
from jax.experimental.pallas import tpu as pltpu
from jax.sharding import PartitionSpec as P

HD = 128
EPS = 1e-05
MESH = pl.DeviceIdType.MESH
F32 = jnp.float32
BF16 = jnp.bfloat16

STRIP = 16
REL = [(0, 0), (0, 1), (1, 0), (3, 0), (1, 1), (3, 1), (2, 0), (2, 1)]


def split_bf16(a):
    hi = a.astype(BF16)
    return hi, (a - hi.astype(F32)).astype(BF16)


def mm3(a, b, dims):
    a_hi, a_lo = split_bf16(a)
    b_hi, b_lo = split_bf16(b)

    def dot(u, w):
        return lax.dot_general(u, w, (dims, ((), ())), preferred_element_type=F32)

    return dot(a_hi, b_hi) + (dot(a_hi, b_lo) + dot(a_lo, b_hi))


NN = ((1,), (0,))
NT = ((1,), (1,))


def heads_to_rows(a):
    return jnp.concatenate([a[:, i : i + HD] for i in range(0, a.shape[1], HD)], axis=0)


def rows_to_heads(a, rows):
    return jnp.concatenate([a[i : i + rows] for i in range(0, a.shape[0], rows)], axis=1)


def softmax_probs(query_rows, keys, rows):
    scores = mm3(query_rows, keys, NT) * HD ** (-0.5)
    row = lax.broadcasted_iota(jnp.int32, (rows, rows), 0)
    col = lax.broadcasted_iota(jnp.int32, (rows, rows), 1)
    causal = jnp.concatenate([row >= col] * (scores.shape[0] // rows), axis=0)
    scores = jnp.where(causal, scores, -1e30)
    expo = jnp.exp(scores - jnp.max(scores, axis=-1, keepdims=True))
    return expo / jnp.sum(expo, axis=-1, keepdims=True)


class Gather:
    strips = {(5, 0): (3, 0), (4, 1): (2, 1)}

    def __init__(self, buf, recv, sent, dev, source, flip):
        self.buf, self.recv, self.sent, self.dev = buf, recv, sent, dev
        self.source, self.flip = source, flip
        self.here = set()

    def copy(self, src, dst, half, to):
        rows = self.buf.shape[2]
        lo = STRIP if (dst, half) in self.strips else 0
        at = pl.ds(lo, rows - lo)
        return pltpu.make_async_remote_copy(
            src_ref=self.buf.at[src, half, at],
            dst_ref=self.buf.at[dst, half, at],
            send_sem=self.sent,
            recv_sem=self.recv.at[dst, half],
            device_id=self.dev(*to),
            device_id_type=MESH,
        )

    def strip(self, dst, half):
        at = pl.ds(0, STRIP)
        src, _ = self.strips[dst, half]
        return pltpu.make_async_remote_copy(
            src_ref=self.buf.at[src, half, at],
            dst_ref=self.buf.at[dst, half, at],
            send_sem=self.sent,
            recv_sem=self.recv.at[0, half],
            device_id=self.dev(0, 1),
            device_id_type=MESH,
        )

    def ready(self, slot, halves=(0, 1)):
        for half in halves:
            if slot and (slot, half) not in self.here:
                self.here.add((slot, half))
                self.copy(slot, slot, half, (0, 1)).wait_recv()
                if (slot, half) in self.strips:
                    self.strip(slot, half).wait_recv()

    def start(self, half):
        self.source(self, half)
        self.copy(0, 1, half, (0, 1)).start()
        self.copy(0, 3, half, (1, 0)).start()
        self.copy(0, 2, 1 - half if self.flip else half, (3, 0)).start()

    def across(self, half):
        self.ready(1, (half,))
        self.copy(1, 5, half, (1, 0)).start()
        self.copy(1, 4, half, (3, 0)).start()

    def along_up(self):
        self.ready(3, (0,))
        self.copy(3, 6, 0, (1, 0)).start()
        self.strip(5, 0).start()

    def along_down(self):
        self.ready(2, (1,))
        self.copy(2, 6, 1, (3, 0)).start()
        self.strip(4, 1).start()

    def last(self, half):
        self.ready(6, (half,))
        self.copy(6, 7, half, (0, 1)).start()

    def drain(self):
        rest = self.buf.at[pl.ds(1, 7)]
        pltpu.make_async_copy(rest, rest, self.sent).wait()


class Scatter:
    def __init__(self, parts, out, got, recv, sent, dev):
        self.parts, self.out, self.got = parts, out, got
        self.recv, self.sent, self.dev = recv, sent, dev
        self.half_rows = out.shape[2]

    def copy(self, slot, half, to, lo=0, hi=None, recv=None):
        at = pl.ds(lo, (hi or self.half_rows) - lo)
        return pltpu.make_async_remote_copy(
            src_ref=self.out.at[slot, half, at],
            dst_ref=self.got.at[slot, half, at],
            send_sem=self.sent,
            recv_sem=self.recv.at[slot if recv is None else recv, half],
            device_id=self.dev(*to),
            device_id_type=MESH,
        )

    def body(self, slot, half, to):
        return self.copy(slot, half, to, STRIP if (slot, half) in Gather.strips else 0)

    def strip(self, slot, half):
        return self.copy(slot, half, (0, 1), 0, STRIP, recv=0)

    def wait(self, slot, half):
        self.body(slot, half, (0, 1)).wait_recv()

    def part(self, slot, half):
        return self.parts[slot, pl.ds(half * self.half_rows, self.half_rows), :]

    def block(self, slot, half, strip):
        if strip is None:
            return self.got[slot, half].astype(F32)
        lo, hi = (0, STRIP) if strip else (STRIP, self.half_rows)
        piece = self.got[slot, half, lo:hi].astype(F32)
        blank = jnp.zeros((self.half_rows - (hi - lo), piece.shape[1]), F32)
        return jnp.concatenate([piece, blank] if strip else [blank, piece], axis=0)

    def push(self, slot, half, to, adds=()):
        total = self.part(slot, half)
        for other, strip in adds:
            total = total + self.block(other, half, strip)
        self.out[slot, half] = total.astype(BF16)
        self.body(slot, half, to).start()
        if (slot, half) in Gather.strips:
            self.strip(slot, half).start()

    def begin(self, slot):
        to = {7: (0, 1), 4: (1, 0), 5: (3, 0), 2: (1, 0), 3: (3, 0)}[slot]
        for half in {2: (0,), 3: (1,)}.get(slot, (0, 1)):
            self.push(slot, half, to)

    def last(self, half):
        self.wait(7, half)
        self.push(6, half, (1, 0) if half else (3, 0), [(7, None)])

    def across(self, half):
        self.wait(4, half)
        self.wait(5, half)
        self.push(1, half, (0, 1), [(4, False if half else None), (5, None if half else False)])

    def along_down(self):
        self.wait(6, 0)
        self.strip(5, 0).wait_recv()
        self.push(3, 0, (3, 0), [(6, None), (5, True)])

    def along_up(self):
        self.wait(6, 1)
        self.strip(4, 1).wait_recv()
        self.push(2, 1, (1, 0), [(6, None), (4, True)])

    def total(self, half):
        for slot in (1, 2, 3):
            self.wait(slot, half)
        total = self.part(0, half)
        for slot in (1, 2, 3):
            total = total + self.got[slot, half].astype(F32)
        return total

    def drain(self):
        rest = self.out.at[pl.ds(1, 7)]
        pltpu.make_async_copy(rest, rest, self.sent).wait()


def kernel(
    act_ref, grad_ref, stash_ref, fresh_ref, head_ref, gain_ref, wq_ref, wk_ref, wv_ref, wo_ref,
    act_out, grad_out,
    w_in, w_out, gains, edges, ag, parts_f, parts_b, outs, gots, acc_f, acc_s, acc_d, sq_f, sq_s,
    mixed_ref, dqkv_ref, moved, totals, total_out,
    ag_recv, ag_sent, rs_recv, rs_sent, tot_recv, tot_sent, recall_send, recall_recv,
    move_send, move_recv, load_sem, w_sem,
):
    n_section = lax.axis_size("section")
    section = lax.axis_index("section")
    tensor = lax.axis_index("tensor")
    place_y, place_z = tensor // 2, lax.rem(tensor, 2)
    half, width = act_ref.shape[1:]
    rows = 2 * half
    q_cols = wq_ref.shape[2]
    k_cols = wk_ref.shape[2]
    full_width = 8 * width

    def owner(dy, dz):
        return lax.rem(place_y + dy, 4) * 2 + lax.rem(place_z + dz, 2)

    def dev(dy, dz):
        return (section, owner(dy, dz))

    def sec(by):
        return (lax.rem(section + by + n_section, n_section), tensor)

    barrier = pltpu.get_barrier_semaphore()
    for dy, dz in REL[1:]:
        pl.semaphore_signal(barrier, inc=1, device_id=dev(dy, dz), device_id_type=MESH)
    for by in (1, -1, n_section // 2):
        pl.semaphore_signal(barrier, inc=1, device_id=sec(by), device_id_type=MESH)

    def own(one, half):
        pass

    def recalled(tick):
        def source(one, half):
            if half == 0:
                recalls[tick].wait_recv()

        return source

    def arrived(index, at_edge):
        def source(one, part):
            shift(index, part, 1).wait_recv()
            edge = edges[index, pl.ds(part * half, half), :]
            one.buf[0, part] = jnp.where(at_edge, edge, moved[index, part])

        return source

    sources = (
        own, own, recalled(0), recalled(1),
        arrived(0, section == 0), arrived(1, section == n_section - 1),
    )
    a0, g0, s0, s1, a1, g1 = [
        Gather(ag.at[i], ag_recv.at[i], ag_sent.at[i], dev, source, i < 4)
        for i, source in enumerate(sources)
    ]
    rs_a0, rs_g0, rs_a1, rs_g1 = [
        Scatter(parts, outs.at[i], gots.at[i], rs_recv.at[i], rs_sent.at[i], dev)
        for i, parts in enumerate((parts_f, parts_b, parts_f, parts_b))
    ]

    loads = [
        pltpu.make_async_copy(act_ref, a0.buf.at[0], load_sem.at[0]),
        pltpu.make_async_copy(grad_ref, g0.buf.at[0], load_sem.at[1]),
    ]
    for slot, (dy, dz) in enumerate(REL):
        loads.append(pltpu.make_async_copy(gain_ref.at[owner(dy, dz)], gains.at[slot], load_sem.at[2]))
    for slot, (dy, dz) in enumerate(REL):
        who = owner(dy, dz)
        loads += [
            pltpu.make_async_copy(wq_ref.at[who], w_in.at[slot, :, pl.ds(0, q_cols)], w_sem.at[0]),
            pltpu.make_async_copy(wk_ref.at[who], w_in.at[slot, :, pl.ds(q_cols, k_cols)], w_sem.at[0]),
            pltpu.make_async_copy(wv_ref.at[who], w_in.at[slot, :, pl.ds(q_cols + k_cols, k_cols)], w_sem.at[0]),
        ]
    for slot, (dy, dz) in enumerate(REL):
        at = pl.ds(pl.multiple_of(owner(dy, dz) * width, width), width)
        loads.append(pltpu.make_async_copy(wo_ref.at[:, at], w_out.at[slot], w_sem.at[1]))
    loads += [
        pltpu.make_async_copy(fresh_ref, edges.at[0], load_sem.at[3]),
        pltpu.make_async_copy(head_ref, edges.at[1], load_sem.at[4]),
    ]
    for load in loads[:10]:
        load.start()
    loads[0].wait()
    loads[1].wait()
    pl.semaphore_wait(barrier, 10)

    recalls = [
        pltpu.make_async_remote_copy(
            src_ref=stash_ref.at[tick],
            dst_ref=one.buf.at[0],
            send_sem=recall_send.at[tick],
            recv_sem=recall_recv.at[tick],
            device_id=sec(n_section // 2),
            device_id_type=MESH,
        )
        for tick, one in enumerate((s0, s1))
    ]

    def shift(index, part, by):
        return pltpu.make_async_remote_copy(
            src_ref=(act_out, grad_out)[index].at[0, part],
            dst_ref=moved.at[index, part],
            send_sem=move_send.at[index, part],
            recv_sem=move_recv.at[index, part],
            device_id=sec(by),
            device_id_type=MESH,
        )

    def clear(*refs):
        for ref in refs:
            ref[...] = jnp.zeros_like(ref)

    def whole(buf, slot):
        return buf[slot].reshape(rows, width)

    def project(one, acc, squares, lo, hi):
        for slot in range(lo, hi):
            one.ready(slot)

        @pl.loop(lo, hi)
        def _(slot):
            x = whole(one.buf, slot).astype(F32)
            square = x * x
            squares[...] += sum(square[:, i : i + HD] for i in range(0, width, HD))
            scaled = (x * gains[slot]).astype(BF16)
            acc[...] += jnp.dot(scaled, w_in[slot], preferred_element_type=F32)

    def pull_mixed(one, lo, hi):
        for slot in range(lo, hi):
            one.ready(slot)

        @pl.loop(lo, hi)
        def _(slot):
            acc_d[...] += lax.dot_general(
                whole(one.buf, slot), w_out[slot], (NT, ((), ())), preferred_element_type=F32
            )

    def inverse_rms(squares):
        mean = jnp.sum(squares, axis=-1, keepdims=True) / full_width
        return lax.rsqrt(mean + EPS)

    def forward_attention():
        qkv = acc_f[...] * inverse_rms(sq_f[...])
        query = heads_to_rows(qkv[:, :q_cols])
        keys = qkv[:, q_cols : q_cols + k_cols]
        values = qkv[:, q_cols + k_cols :]
        probs = softmax_probs(query, keys, rows)
        mixed_ref[...] = rows_to_heads(mm3(probs, values, NN), rows).astype(BF16)

    def forward_parts(lo, hi):
        @pl.loop(lo, hi)
        def _(slot):
            parts_f[slot] = jnp.dot(mixed_ref[...], w_out[slot], preferred_element_type=F32)

    def backward_parts(lo, hi):
        @pl.loop(lo, hi)
        def _(slot):
            parts_b[slot] = lax.dot_general(
                dqkv_ref[...], w_in[slot], (NT, ((), ())), preferred_element_type=F32
            )

    def diagonal():
        row = lax.broadcasted_iota(jnp.int32, (rows, rows), 0)
        col = lax.broadcasted_iota(jnp.int32, (rows, rows), 1)
        return row == col

    def total_copy(tick, mirror, dy, dz):
        return pltpu.make_async_remote_copy(
            src_ref=total_out.at[tick],
            dst_ref=totals.at[tick, mirror],
            send_sem=tot_sent.at[tick],
            recv_sem=tot_recv.at[tick, mirror],
            device_id=dev(dy, dz),
            device_id_type=MESH,
        )

    def backward_attention(tick):
        raw = acc_s[tick]
        qkv = raw * inverse_rms(sq_s[tick])
        query = heads_to_rows(qkv[:, :q_cols])
        keys = qkv[:, q_cols : q_cols + k_cols]
        values = qkv[:, q_cols + k_cols :]
        probs = softmax_probs(query, keys, rows)
        d_mixed = heads_to_rows(acc_d[...])
        d_values = mm3(probs.T, d_mixed, NN)
        d_probs = mm3(d_mixed, values, NT)
        d_scores = probs * (d_probs - jnp.sum(d_probs * probs, axis=-1, keepdims=True))
        d_scores = d_scores * HD ** (-0.5)
        d_query = rows_to_heads(mm3(d_scores, keys, NN), rows)
        d_keys = mm3(d_scores.T, query, NN)
        dqkv = jnp.concatenate([d_query, d_keys, d_values], axis=1).astype(BF16)
        dqkv_ref[...] = dqkv
        share = jnp.sum(dqkv.astype(F32) * raw, axis=-1, keepdims=True)
        line = jnp.sum(jnp.where(diagonal(), share, 0.0), axis=0, keepdims=True)
        total_out[tick] = jnp.broadcast_to(line, total_out.shape[1:])

    def send_totals(tick):
        for dy, dz in REL[1:]:
            total_copy(tick, REL.index(((4 - dy) % 4, dz)), dy, dz).start()

    def act_finish(tick, one, rs, i):
        out = (one.buf[0, i].astype(F32) + rs.total(i)).astype(BF16)
        act_out[tick, i] = out
        if tick == 0:
            shift(0, i, 1).start()

    def grad_finish(tick, one, stashed, rs, i):
        if i == 0:
            for slot in range(1, 8):
                total_copy(tick, slot, 0, 1).wait_recv()
        line = total_out[tick]
        for slot in range(1, 8):
            line = line + totals[tick, slot]
        full = jnp.where(diagonal(), line[0:1, :], 0.0)
        cut = slice(i * half, (i + 1) * half)
        row_total = jnp.sum(full[cut], axis=-1, keepdims=True)
        inv = inverse_rms(sq_s[tick, pl.ds(i * half, half), :])
        x = stashed.buf[0, i].astype(F32)
        scaled = rs.total(i) * gains[0]
        out = (
            one.buf[0, i].astype(F32)
            + inv * scaled
            - x * (inv * inv * inv) * row_total / full_width
        ).astype(BF16)
        grad_out[tick, i] = out
        if tick == 0:
            shift(1, i, -1).start()

    def start_loads():
        for load in loads[10:]:
            load.start()
        recalls[0].start()
        recalls[1].start()

    def wait_weights():
        for buf, sem in ((gains, load_sem.at[2]), (w_in, w_sem.at[0]), (w_out, w_sem.at[1])):
            pltpu.make_async_copy(buf, buf, sem).wait()
        loads[-2].wait()
        loads[-1].wait()

    a0.start(0)
    a0.start(1)
    start_loads()
    g0.start(0)
    a0.along_up()
    a0.along_down()
    s0.start(0)
    s0.start(1)
    g0.start(1)
    clear(acc_f, acc_s, acc_d, sq_f, sq_s)
    wait_weights()
    pull_mixed(g0, 0, 1)
    project(a0, acc_f, sq_f, 0, 1)
    project(s0, acc_s.at[0], sq_s.at[0], 0, 1)
    g0.along_down()
    a0.last(0)
    g0.along_up()
    a0.across(0)
    s0.along_down()
    a0.across(1)
    a0.last(1)
    project(a0, acc_f, sq_f, 6, 7)
    s0.along_up()
    project(s0, acc_s.at[0], sq_s.at[0], 2, 3)
    pull_mixed(g0, 1, 2)
    s0.across(0)
    s0.across(1)
    g0.last(0)
    pull_mixed(g0, 6, 7)
    pull_mixed(g0, 2, 3)
    g0.last(1)
    project(a0, acc_f, sq_f, 2, 4)
    g0.across(0)
    project(s0, acc_s.at[0], sq_s.at[0], 1, 2)
    project(s0, acc_s.at[0], sq_s.at[0], 3, 4)
    s0.last(1)
    pull_mixed(g0, 3, 4)
    project(a0, acc_f, sq_f, 7, 8)
    g0.across(1)
    project(a0, acc_f, sq_f, 1, 2)
    s0.last(0)
    project(a0, acc_f, sq_f, 4, 6)
    forward_attention()
    clear(acc_f, sq_f)
    forward_parts(7, 8)
    rs_a0.begin(7)
    s1.start(0)
    forward_parts(4, 5)
    rs_a0.begin(4)
    forward_parts(5, 6)
    rs_a0.begin(5)
    forward_parts(6, 7)
    forward_parts(3, 4)
    rs_a0.begin(3)
    pull_mixed(g0, 7, 8)
    s1.start(1)
    project(s0, acc_s.at[0], sq_s.at[0], 6, 7)
    project(s0, acc_s.at[0], sq_s.at[0], 4, 5)
    project(s0, acc_s.at[0], sq_s.at[0], 7, 8)
    pull_mixed(g0, 4, 5)
    project(s0, acc_s.at[0], sq_s.at[0], 5, 6)
    pull_mixed(g0, 5, 6)
    backward_attention(0)
    send_totals(0)
    forward_parts(2, 3)
    rs_a0.last(1)
    rs_a0.last(0)
    backward_parts(7, 8)
    backward_parts(5, 6)
    rs_g0.begin(7)
    rs_a0.begin(2)
    backward_parts(1, 2)
    rs_g0.begin(5)
    backward_parts(4, 5)
    backward_parts(6, 7)
    rs_g0.begin(4)
    forward_parts(1, 2)
    rs_a0.across(1)
    project(s1, acc_s.at[1], sq_s.at[1], 0, 1)
    project(s1, acc_s.at[1], sq_s.at[1], 3, 4)
    rs_g0.last(0)
    backward_parts(3, 4)
    rs_a0.along_up()
    rs_a0.along_down()
    rs_a0.across(0)
    rs_g0.last(1)
    project(s1, acc_s.at[1], sq_s.at[1], 1, 2)
    s1.along_up()
    rs_g0.begin(3)
    rs_g0.across(0)
    rs_g0.across(1)
    backward_parts(2, 3)
    rs_g0.begin(2)
    rs_g0.along_down()
    forward_parts(0, 1)
    act_finish(0, a0, rs_a0, 0)
    s1.along_down()
    backward_parts(0, 1)
    act_finish(0, a0, rs_a0, 1)
    rs_g0.along_up()
    s1.across(0)
    s1.across(1)
    s1.last(0)
    grad_finish(0, g0, s0, rs_g0, 0)
    grad_finish(0, g0, s0, rs_g0, 1)
    a1.start(0)
    a1.start(1)
    g1.start(0)
    a1.along_up()
    g1.start(1)
    clear(acc_d)
    pull_mixed(g1, 0, 1)
    project(s1, acc_s.at[1], sq_s.at[1], 4, 5)
    a1.along_down()
    g1.along_up()
    s1.last(1)
    project(s1, acc_s.at[1], sq_s.at[1], 6, 7)
    a1.across(0)
    project(a1, acc_f, sq_f, 0, 1)
    project(a1, acc_f, sq_f, 2, 4)
    a1.last(0)
    g1.along_down()
    a1.across(1)
    pull_mixed(g1, 1, 2)
    a1.last(1)
    project(s1, acc_s.at[1], sq_s.at[1], 5, 6)
    pull_mixed(g1, 2, 3)
    project(a1, acc_f, sq_f, 1, 2)
    g1.across(0)
    g1.across(1)
    project(s1, acc_s.at[1], sq_s.at[1], 7, 8)
    g1.last(0)
    project(s1, acc_s.at[1], sq_s.at[1], 2, 3)
    project(a1, acc_f, sq_f, 6, 7)
    pull_mixed(g1, 3, 4)
    pull_mixed(g1, 6, 7)
    g1.last(1)
    project(a1, acc_f, sq_f, 4, 6)
    project(a1, acc_f, sq_f, 7, 8)
    forward_attention()
    forward_parts(5, 6)
    rs_a1.begin(5)
    forward_parts(4, 5)
    rs_a1.begin(4)
    forward_parts(7, 8)
    forward_parts(2, 3)
    rs_a1.begin(2)
    rs_a1.begin(7)
    forward_parts(3, 4)
    pull_mixed(g1, 5, 6)
    rs_a1.begin(3)
    pull_mixed(g1, 4, 5)
    pull_mixed(g1, 7, 8)
    backward_attention(1)
    backward_parts(7, 8)
    rs_g1.begin(7)
    backward_parts(5, 6)
    rs_g1.begin(5)
    backward_parts(4, 5)
    rs_g1.begin(4)
    forward_parts(6, 7)
    rs_a1.last(0)
    rs_a1.last(1)
    backward_parts(0, 1)
    backward_parts(3, 4)
    backward_parts(1, 2)
    backward_parts(6, 7)
    rs_g1.last(0)
    forward_parts(1, 2)
    rs_a1.across(1)
    rs_g1.last(1)
    rs_g1.across(0)
    backward_parts(2, 3)
    rs_g1.begin(3)
    rs_g1.across(1)
    send_totals(1)
    rs_g1.begin(2)
    rs_a1.along_down()
    rs_a1.across(0)
    rs_a1.along_up()
    rs_g1.along_down()
    rs_g1.along_up()
    forward_parts(0, 1)
    act_finish(1, a1, rs_a1, 0)
    act_finish(1, a1, rs_a1, 1)
    grad_finish(1, g1, s1, rs_g1, 0)
    grad_finish(1, g1, s1, rs_g1, 1)

    for one in (a0, g0, s0, s1, a1, g1, rs_a0, rs_g0, rs_a1, rs_g1):
        one.drain()
    for tick in range(2):
        rest = totals.at[tick, pl.ds(1, 7)]
        pltpu.make_async_copy(rest, rest, tot_sent.at[tick]).wait()
    for one in recalls:
        one.wait_send()
    for i in range(2):
        shift(0, i, 1).wait_send()
        shift(1, i, -1).wait_send()


def per_device(
    act_in, grad_in, held_stash, new_batch, head_grad, norm_gain, w_query, w_key, w_value, w_out
):
    rows, width = act_in.shape[1:]
    half = rows // 2
    q_cols, k_cols = w_query.shape[2], w_key.shape[2]
    cols = q_cols + 2 * k_cols
    vmem = pl.BlockSpec(memory_space=pltpu.VMEM)
    hbm = pl.BlockSpec(memory_space=pl.ANY)
    out = pltpu.VMEM((2, 2, half, width), BF16)
    scratch = [
        pltpu.VMEM((8, width, cols), BF16),
        pltpu.VMEM((8, q_cols, width), BF16),
        pltpu.VMEM((8, 1, width), F32),
        pltpu.VMEM((2, rows, width), BF16),
        pltpu.VMEM((6, 8, 2, half, width), BF16),
        pltpu.VMEM((8, rows, width), F32),
        pltpu.VMEM((8, rows, width), F32),
        pltpu.VMEM((4, 8, 2, half, width), BF16),
        pltpu.VMEM((4, 8, 2, half, width), BF16),
        pltpu.VMEM((rows, cols), F32),
        pltpu.VMEM((2, rows, cols), F32),
        pltpu.VMEM((rows, q_cols), F32),
        pltpu.VMEM((rows, HD), F32),
        pltpu.VMEM((2, rows, HD), F32),
        pltpu.VMEM((rows, q_cols), BF16),
        pltpu.VMEM((rows, cols), BF16),
        pltpu.VMEM((2, 2, half, width), BF16),
        pltpu.VMEM((2, 8, 8, rows), F32),
        pltpu.VMEM((2, 8, rows), F32),
        pltpu.SemaphoreType.DMA((6, 8, 2)),
        pltpu.SemaphoreType.DMA((6,)),
        pltpu.SemaphoreType.DMA((4, 8, 2)),
        pltpu.SemaphoreType.DMA((4,)),
        pltpu.SemaphoreType.DMA((2, 8)),
        pltpu.SemaphoreType.DMA((2,)),
        pltpu.SemaphoreType.DMA((2,)),
        pltpu.SemaphoreType.DMA((2,)),
        pltpu.SemaphoreType.DMA((2, 2)),
        pltpu.SemaphoreType.DMA((2, 2)),
        pltpu.SemaphoreType.DMA((5,)),
        pltpu.SemaphoreType.DMA((2,)),
    ]
    acts, grads = pl.pallas_call(
        kernel,
        out_shape=(out, out),
        in_specs=[hbm] * 10,
        out_specs=(vmem, vmem),
        scratch_shapes=scratch,
        compiler_params=pltpu.CompilerParams(
            collective_id=0, has_side_effects=True, vmem_limit_bytes=60 << 20
        ),
    )(
        act_in.reshape(2, half, width),
        grad_in.reshape(2, half, width),
        held_stash.reshape(2, 2, half, width),
        new_batch,
        head_grad,
        norm_gain.reshape(8, 1, width),
        w_query.reshape(8, width, q_cols),
        w_key.reshape(8, width, k_cols),
        w_value.reshape(8, width, k_cols),
        w_out[0],
    )
    shape = (1, 2, rows, width)
    return acts.reshape(shape), grads.reshape(shape)


def solution(mesh):
    in_specs = (
        P("section", None, "tensor"),
        P("section", None, "tensor"),
        P("section", None, None, "tensor"),
        P(None, "tensor"),
        P(None, "tensor"),
        P("section", None),
        P("section", None, "tensor"),
        P("section", None, "tensor"),
        P("section", None, "tensor"),
        P("section", "tensor", None),
    )
    out_specs = (P("section", None, None, "tensor"), P("section", None, None, "tensor"))
    return jax.shard_map(
        per_device, mesh=mesh, in_specs=in_specs, out_specs=out_specs, check_vma=False
    )
```

```python
import functools

import jax
import jax.numpy as jnp
from jax import lax
from jax.experimental import pallas as pl
from jax.experimental.pallas import tpu as pltpu
from jax.sharding import PartitionSpec as P

HD = 128
EPS = 1e-05
MESH = pl.DeviceIdType.MESH
F32 = jnp.float32
BF16 = jnp.bfloat16

STRIP = 16
REL = [(0, 0), (0, 1), (1, 0), (3, 0), (1, 1), (3, 1), (2, 0), (2, 1)]


def split_bf16(a):
    hi = a.astype(BF16)
    return hi, (a - hi.astype(F32)).astype(BF16)


def mm3(a, b, dims):
    a_hi, a_lo = split_bf16(a)
    b_hi, b_lo = split_bf16(b)

    def dot(u, w):
        return lax.dot_general(u, w, (dims, ((), ())), preferred_element_type=F32)

    return dot(a_hi, b_hi) + (dot(a_hi, b_lo) + dot(a_lo, b_hi))


NN = ((1,), (0,))
NT = ((1,), (1,))


def heads_to_rows(a):
    return jnp.concatenate([a[:, i : i + HD] for i in range(0, a.shape[1], HD)], axis=0)


def rows_to_heads(a, rows):
    return jnp.concatenate([a[i : i + rows] for i in range(0, a.shape[0], rows)], axis=1)


def softmax_probs(query_rows, keys, rows):
    scores = mm3(query_rows, keys, NT) * HD ** (-0.5)
    row = lax.broadcasted_iota(jnp.int32, (rows, rows), 0)
    col = lax.broadcasted_iota(jnp.int32, (rows, rows), 1)
    causal = jnp.concatenate([row >= col] * (scores.shape[0] // rows), axis=0)
    scores = jnp.where(causal, scores, -1e30)
    expo = jnp.exp(scores - jnp.max(scores, axis=-1, keepdims=True))
    return expo / jnp.sum(expo, axis=-1, keepdims=True)


class Gather:
    strips = {(5, 0): (3, 0), (4, 1): (2, 1)}

    def __init__(self, buf, recv, sent, dev, source, flip):
        self.buf, self.recv, self.sent, self.dev = buf, recv, sent, dev
        self.source, self.flip = source, flip
        self.here = set()

    def copy(self, src, dst, half, to):
        rows = self.buf.shape[2]
        lo = STRIP if (dst, half) in self.strips else 0
        at = pl.ds(lo, rows - lo)
        return pltpu.make_async_remote_copy(
            src_ref=self.buf.at[src, half, at],
            dst_ref=self.buf.at[dst, half, at],
            send_sem=self.sent,
            recv_sem=self.recv.at[dst, half],
            device_id=self.dev(*to),
            device_id_type=MESH,
        )

    def strip(self, dst, half):
        at = pl.ds(0, STRIP)
        src, _ = self.strips[dst, half]
        return pltpu.make_async_remote_copy(
            src_ref=self.buf.at[src, half, at],
            dst_ref=self.buf.at[dst, half, at],
            send_sem=self.sent,
            recv_sem=self.recv.at[0, half],
            device_id=self.dev(0, 1),
            device_id_type=MESH,
        )

    def ready(self, slot, halves=(0, 1)):
        for half in halves:
            if slot and (slot, half) not in self.here:
                self.here.add((slot, half))
                self.copy(slot, slot, half, (0, 1)).wait_recv()
                if (slot, half) in self.strips:
                    self.strip(slot, half).wait_recv()

    def start(self, half):
        self.source(self, half)
        self.copy(0, 1, half, (0, 1)).start()
        self.copy(0, 3, half, (1, 0)).start()
        self.copy(0, 2, 1 - half if self.flip else half, (3, 0)).start()

    def across(self, half):
        self.ready(1, (half,))
        self.copy(1, 5, half, (1, 0)).start()
        self.copy(1, 4, half, (3, 0)).start()

    def along_up(self):
        self.ready(3, (0,))
        self.copy(3, 6, 0, (1, 0)).start()
        self.strip(5, 0).start()

    def along_down(self):
        self.ready(2, (1,))
        self.copy(2, 6, 1, (3, 0)).start()
        self.strip(4, 1).start()

    def last(self, half):
        self.ready(6, (half,))
        self.copy(6, 7, half, (0, 1)).start()

    def drain(self):
        rest = self.buf.at[pl.ds(1, 7)]
        pltpu.make_async_copy(rest, rest, self.sent).wait()


class Scatter:
    def __init__(self, parts, out, got, recv, sent, dev):
        self.parts, self.out, self.got = parts, out, got
        self.recv, self.sent, self.dev = recv, sent, dev
        self.half_rows = out.shape[2]

    def copy(self, slot, half, to, lo=0, hi=None, recv=None):
        at = pl.ds(lo, (hi or self.half_rows) - lo)
        return pltpu.make_async_remote_copy(
            src_ref=self.out.at[slot, half, at],
            dst_ref=self.got.at[slot, half, at],
            send_sem=self.sent,
            recv_sem=self.recv.at[slot if recv is None else recv, half],
            device_id=self.dev(*to),
            device_id_type=MESH,
        )

    def body(self, slot, half, to):
        return self.copy(slot, half, to, STRIP if (slot, half) in Gather.strips else 0)

    def strip(self, slot, half):
        return self.copy(slot, half, (0, 1), 0, STRIP, recv=0)

    def wait(self, slot, half):
        self.body(slot, half, (0, 1)).wait_recv()

    def part(self, slot, half):
        return self.parts[slot, pl.ds(half * self.half_rows, self.half_rows), :]

    def block(self, slot, half, strip):
        if strip is None:
            return self.got[slot, half].astype(F32)
        lo, hi = (0, STRIP) if strip else (STRIP, self.half_rows)
        piece = self.got[slot, half, lo:hi].astype(F32)
        blank = jnp.zeros((self.half_rows - (hi - lo), piece.shape[1]), F32)
        return jnp.concatenate([piece, blank] if strip else [blank, piece], axis=0)

    def push(self, slot, half, to, adds=()):
        total = self.part(slot, half)
        for other, strip in adds:
            total = total + self.block(other, half, strip)
        self.out[slot, half] = total.astype(BF16)
        self.body(slot, half, to).start()
        if (slot, half) in Gather.strips:
            self.strip(slot, half).start()

    def begin(self, slot):
        to = {7: (0, 1), 4: (1, 0), 5: (3, 0), 2: (1, 0), 3: (3, 0)}[slot]
        for half in {2: (0,), 3: (1,)}.get(slot, (0, 1)):
            self.push(slot, half, to)

    def last(self, half):
        self.wait(7, half)
        self.push(6, half, (1, 0) if half else (3, 0), [(7, None)])

    def across(self, half):
        self.wait(4, half)
        self.wait(5, half)
        self.push(1, half, (0, 1), [(4, False if half else None), (5, None if half else False)])

    def along_down(self):
        self.wait(6, 0)
        self.strip(5, 0).wait_recv()
        self.push(3, 0, (3, 0), [(6, None), (5, True)])

    def along_up(self):
        self.wait(6, 1)
        self.strip(4, 1).wait_recv()
        self.push(2, 1, (1, 0), [(6, None), (4, True)])

    def total(self, half):
        for slot in (1, 2, 3):
            self.wait(slot, half)
        total = self.part(0, half)
        for slot in (1, 2, 3):
            total = total + self.got[slot, half].astype(F32)
        return total

    def drain(self):
        rest = self.out.at[pl.ds(1, 7)]
        pltpu.make_async_copy(rest, rest, self.sent).wait()


def kernel(
    act_ref, grad_ref, stash_ref, fresh_ref, head_ref, gain_ref, wq_ref, wk_ref, wv_ref, wo_ref,
    act_out, grad_out,
    w_in, w_out, gains, edges, ag, parts_f, parts_b, outs, gots, acc_f, acc_s, acc_d, sq_f, sq_s,
    mixed_ref, dqkv_ref, moved, totals, total_out,
    ag_recv, ag_sent, rs_recv, rs_sent, tot_recv, tot_sent, recall_send, recall_recv,
    move_send, move_recv, load_sem, w_sem,
):
    n_section = lax.axis_size("section")
    section = lax.axis_index("section")
    tensor = lax.axis_index("tensor")
    place_y, place_z = tensor // 2, lax.rem(tensor, 2)
    half, width = act_ref.shape[1:]
    rows = 2 * half
    q_cols = wq_ref.shape[2]
    k_cols = wk_ref.shape[2]
    full_width = 8 * width

    def owner(dy, dz):
        return lax.rem(place_y + dy, 4) * 2 + lax.rem(place_z + dz, 2)

    def dev(dy, dz):
        return (section, owner(dy, dz))

    def sec(by):
        return (lax.rem(section + by + n_section, n_section), tensor)

    barrier = pltpu.get_barrier_semaphore()
    for dy, dz in REL[1:]:
        pl.semaphore_signal(barrier, inc=1, device_id=dev(dy, dz), device_id_type=MESH)
    for by in (1, -1, n_section // 2):
        pl.semaphore_signal(barrier, inc=1, device_id=sec(by), device_id_type=MESH)

    def own(one, half):
        pass

    def recalled(tick):
        def source(one, half):
            if half == 0:
                recalls[tick].wait_recv()

        return source

    def arrived(index, at_edge):
        def source(one, part):
            shift(index, part, 1).wait_recv()
            edge = edges[index, pl.ds(part * half, half), :]
            one.buf[0, part] = jnp.where(at_edge, edge, moved[index, part])

        return source

    sources = (
        own, own, recalled(0), recalled(1),
        arrived(0, section == 0), arrived(1, section == n_section - 1),
    )
    a0, g0, s0, s1, a1, g1 = [
        Gather(ag.at[i], ag_recv.at[i], ag_sent.at[i], dev, source, i < 4)
        for i, source in enumerate(sources)
    ]
    rs_a0, rs_g0, rs_a1, rs_g1 = [
        Scatter(parts, outs.at[i], gots.at[i], rs_recv.at[i], rs_sent.at[i], dev)
        for i, parts in enumerate((parts_f, parts_b, parts_f, parts_b))
    ]

    loads = [
        pltpu.make_async_copy(act_ref, a0.buf.at[0], load_sem.at[0]),
        pltpu.make_async_copy(grad_ref, g0.buf.at[0], load_sem.at[1]),
    ]
    for slot, (dy, dz) in enumerate(REL):
        loads.append(pltpu.make_async_copy(gain_ref.at[owner(dy, dz)], gains.at[slot], load_sem.at[2]))
    for slot, (dy, dz) in enumerate(REL):
        who = owner(dy, dz)
        loads += [
            pltpu.make_async_copy(wq_ref.at[who], w_in.at[slot, :, pl.ds(0, q_cols)], w_sem.at[0]),
            pltpu.make_async_copy(wk_ref.at[who], w_in.at[slot, :, pl.ds(q_cols, k_cols)], w_sem.at[0]),
            pltpu.make_async_copy(wv_ref.at[who], w_in.at[slot, :, pl.ds(q_cols + k_cols, k_cols)], w_sem.at[0]),
        ]
    for slot, (dy, dz) in enumerate(REL):
        at = pl.ds(pl.multiple_of(owner(dy, dz) * width, width), width)
        loads.append(pltpu.make_async_copy(wo_ref.at[:, at], w_out.at[slot], w_sem.at[1]))
    loads += [
        pltpu.make_async_copy(fresh_ref, edges.at[0], load_sem.at[3]),
        pltpu.make_async_copy(head_ref, edges.at[1], load_sem.at[4]),
    ]
    for load in loads[:10]:
        load.start()
    loads[0].wait()
    loads[1].wait()
    pl.semaphore_wait(barrier, 10)

    recalls = [
        pltpu.make_async_remote_copy(
            src_ref=stash_ref.at[tick],
            dst_ref=one.buf.at[0],
            send_sem=recall_send.at[tick],
            recv_sem=recall_recv.at[tick],
            device_id=sec(n_section // 2),
            device_id_type=MESH,
        )
        for tick, one in enumerate((s0, s1))
    ]

    def shift(index, part, by):
        return pltpu.make_async_remote_copy(
            src_ref=(act_out, grad_out)[index].at[0, part],
            dst_ref=moved.at[index, part],
            send_sem=move_send.at[index, part],
            recv_sem=move_recv.at[index, part],
            device_id=sec(by),
            device_id_type=MESH,
        )

    def clear(*refs):
        for ref in refs:
            ref[...] = jnp.zeros_like(ref)

    def whole(buf, slot):
        return buf[slot].reshape(rows, width)

    def project(one, acc, squares, lo, hi):
        for slot in range(lo, hi):
            one.ready(slot)

        @pl.loop(lo, hi)
        def _(slot):
            x = whole(one.buf, slot).astype(F32)
            square = x * x
            squares[...] += sum(square[:, i : i + HD] for i in range(0, width, HD))
            scaled = (x * gains[slot]).astype(BF16)
            acc[...] += jnp.dot(scaled, w_in[slot], preferred_element_type=F32)

    def pull_mixed(one, lo, hi):
        for slot in range(lo, hi):
            one.ready(slot)

        @pl.loop(lo, hi)
        def _(slot):
            acc_d[...] += lax.dot_general(
                whole(one.buf, slot), w_out[slot], (NT, ((), ())), preferred_element_type=F32
            )

    def inverse_rms(squares):
        mean = jnp.sum(squares, axis=-1, keepdims=True) / full_width
        return lax.rsqrt(mean + EPS)

    def forward_attention():
        qkv = acc_f[...] * inverse_rms(sq_f[...])
        query = heads_to_rows(qkv[:, :q_cols])
        keys = qkv[:, q_cols : q_cols + k_cols]
        values = qkv[:, q_cols + k_cols :]
        probs = softmax_probs(query, keys, rows)
        mixed_ref[...] = rows_to_heads(mm3(probs, values, NN), rows).astype(BF16)

    def forward_parts(lo, hi):
        @pl.loop(lo, hi)
        def _(slot):
            parts_f[slot] = jnp.dot(mixed_ref[...], w_out[slot], preferred_element_type=F32)

    def backward_parts(lo, hi):
        @pl.loop(lo, hi)
        def _(slot):
            parts_b[slot] = lax.dot_general(
                dqkv_ref[...], w_in[slot], (NT, ((), ())), preferred_element_type=F32
            )

    def diagonal():
        row = lax.broadcasted_iota(jnp.int32, (rows, rows), 0)
        col = lax.broadcasted_iota(jnp.int32, (rows, rows), 1)
        return row == col

    def total_copy(tick, mirror, dy, dz):
        return pltpu.make_async_remote_copy(
            src_ref=total_out.at[tick],
            dst_ref=totals.at[tick, mirror],
            send_sem=tot_sent.at[tick],
            recv_sem=tot_recv.at[tick, mirror],
            device_id=dev(dy, dz),
            device_id_type=MESH,
        )

    def backward_attention(tick):
        raw = acc_s[tick]
        qkv = raw * inverse_rms(sq_s[tick])
        query = heads_to_rows(qkv[:, :q_cols])
        keys = qkv[:, q_cols : q_cols + k_cols]
        values = qkv[:, q_cols + k_cols :]
        probs = softmax_probs(query, keys, rows)
        d_mixed = heads_to_rows(acc_d[...])
        d_values = mm3(probs.T, d_mixed, NN)
        d_probs = mm3(d_mixed, values, NT)
        d_scores = probs * (d_probs - jnp.sum(d_probs * probs, axis=-1, keepdims=True))
        d_scores = d_scores * HD ** (-0.5)
        d_query = rows_to_heads(mm3(d_scores, keys, NN), rows)
        d_keys = mm3(d_scores.T, query, NN)
        dqkv = jnp.concatenate([d_query, d_keys, d_values], axis=1).astype(BF16)
        dqkv_ref[...] = dqkv
        share = jnp.sum(dqkv.astype(F32) * raw, axis=-1, keepdims=True)
        line = jnp.sum(jnp.where(diagonal(), share, 0.0), axis=0, keepdims=True)
        total_out[tick] = jnp.broadcast_to(line, total_out.shape[1:])

    def send_totals(tick):
        for dy, dz in REL[1:]:
            total_copy(tick, REL.index(((4 - dy) % 4, dz)), dy, dz).start()

    def act_finish(tick, one, rs, i):
        out = (one.buf[0, i].astype(F32) + rs.total(i)).astype(BF16)
        act_out[tick, i] = out
        if tick == 0:
            shift(0, i, 1).start()

    def grad_finish(tick, one, stashed, rs, i):
        if i == 0:
            for slot in range(1, 8):
                total_copy(tick, slot, 0, 1).wait_recv()
        line = total_out[tick]
        for slot in range(1, 8):
            line = line + totals[tick, slot]
        full = jnp.where(diagonal(), line[0:1, :], 0.0)
        cut = slice(i * half, (i + 1) * half)
        row_total = jnp.sum(full[cut], axis=-1, keepdims=True)
        inv = inverse_rms(sq_s[tick, pl.ds(i * half, half), :])
        x = stashed.buf[0, i].astype(F32)
        scaled = rs.total(i) * gains[0]
        out = (
            one.buf[0, i].astype(F32)
            + inv * scaled
            - x * (inv * inv * inv) * row_total / full_width
        ).astype(BF16)
        grad_out[tick, i] = out
        if tick == 0:
            shift(1, i, -1).start()

    def start_loads():
        recalls[0].start()
        recalls[1].start()
        for load in loads[10:]:
            load.start()

    def wait_weights():
        for buf, sem in ((gains, load_sem.at[2]), (w_in, w_sem.at[0]), (w_out, w_sem.at[1])):
            pltpu.make_async_copy(buf, buf, sem).wait()
        loads[-2].wait()
        loads[-1].wait()

    a0.start(0)
    a0.start(1)
    start_loads()
    g0.start(0)
    g0.start(1)
    s0.start(0)
    wait_weights()
    a0.along_up()
    a0.along_down()
    g0.along_up()
    g0.along_down()
    s0.start(1)
    s0.along_down()
    s0.along_up()
    clear(acc_f, acc_s, acc_d, sq_f, sq_s)
    project(a0, acc_f, sq_f, 0, 1)
    a0.last(0)
    a0.last(1)
    pull_mixed(g0, 0, 2)
    g0.last(1)
    project(a0, acc_f, sq_f, 1, 2)
    a0.across(0)
    a0.across(1)
    project(a0, acc_f, sq_f, 3, 4)
    pull_mixed(g0, 3, 4)
    g0.across(0)
    g0.across(1)
    pull_mixed(g0, 2, 3)
    g0.last(0)
    s0.last(0)
    s0.across(0)
    s0.last(1)
    project(a0, acc_f, sq_f, 2, 3)
    pull_mixed(g0, 6, 7)
    s0.across(1)
    project(a0, acc_f, sq_f, 7, 8)
    project(s0, acc_s.at[0], sq_s.at[0], 0, 2)
    project(a0, acc_f, sq_f, 6, 7)
    project(a0, acc_f, sq_f, 4, 6)
    forward_attention()
    forward_parts(2, 3)
    forward_parts(7, 8)
    project(s0, acc_s.at[0], sq_s.at[0], 2, 3)
    rs_a0.begin(7)
    forward_parts(4, 5)
    rs_a0.begin(4)
    s1.start(0)
    forward_parts(3, 4)
    project(s0, acc_s.at[0], sq_s.at[0], 6, 7)
    s1.start(1)
    pull_mixed(g0, 5, 6)
    pull_mixed(g0, 7, 8)
    pull_mixed(g0, 4, 5)
    forward_parts(1, 2)
    forward_parts(5, 7)
    rs_a0.begin(3)
    rs_a0.begin(5)
    project(s0, acc_s.at[0], sq_s.at[0], 7, 8)
    project(s0, acc_s.at[0], sq_s.at[0], 5, 6)
    project(s0, acc_s.at[0], sq_s.at[0], 3, 5)
    backward_attention(0)
    send_totals(0)
    rs_a0.last(1)
    rs_a0.last(0)
    backward_parts(3, 4)
    backward_parts(7, 8)
    forward_parts(0, 1)
    backward_parts(4, 5)
    rs_g0.begin(4)
    rs_g0.begin(7)
    rs_a0.begin(2)
    backward_parts(5, 6)
    rs_g0.begin(5)
    rs_a0.across(0)
    rs_a0.along_up()
    backward_parts(6, 7)
    rs_g0.last(0)
    rs_a0.across(1)
    rs_a0.along_down()
    project(s1, acc_s.at[1], sq_s.at[1], 0, 1)
    rs_g0.last(1)
    s1.along_up()
    project(s1, acc_s.at[1], sq_s.at[1], 2, 3)
    backward_parts(1, 2)
    rs_g0.across(1)
    backward_parts(2, 3)
    rs_g0.begin(2)
    rs_g0.across(0)
    rs_g0.begin(3)
    rs_g0.along_down()
    s1.along_down()
    rs_g0.along_up()
    act_finish(0, a0, rs_a0, 0)
    act_finish(0, a0, rs_a0, 1)
    backward_parts(0, 1)
    clear(acc_f, sq_f)
    s1.last(0)
    s1.across(0)
    s1.across(1)
    grad_finish(0, g0, s0, rs_g0, 0)
    grad_finish(0, g0, s0, rs_g0, 1)
    clear(acc_d)
    a1.start(0)
    a1.start(1)
    g1.start(0)
    a1.along_up()
    g1.start(1)
    s1.last(1)
    project(s1, acc_s.at[1], sq_s.at[1], 3, 4)
    a1.along_down()
    project(a1, acc_f, sq_f, 0, 2)
    g1.along_up()
    a1.across(0)
    project(s1, acc_s.at[1], sq_s.at[1], 5, 6)
    g1.along_down()
    project(s1, acc_s.at[1], sq_s.at[1], 6, 7)
    project(a1, acc_f, sq_f, 2, 3)
    a1.last(0)
    project(s1, acc_s.at[1], sq_s.at[1], 1, 2)
    a1.across(1)
    a1.last(1)
    pull_mixed(g1, 0, 1)
    pull_mixed(g1, 1, 3)
    g1.across(0)
    project(a1, acc_f, sq_f, 3, 4)
    g1.across(1)
    g1.last(0)
    project(a1, acc_f, sq_f, 6, 7)
    project(s1, acc_s.at[1], sq_s.at[1], 4, 5)
    project(s1, acc_s.at[1], sq_s.at[1], 7, 8)
    pull_mixed(g1, 3, 4)
    g1.last(1)
    pull_mixed(g1, 6, 7)
    project(a1, acc_f, sq_f, 4, 6)
    project(a1, acc_f, sq_f, 7, 8)
    forward_attention()
    forward_parts(4, 5)
    rs_a1.begin(4)
    forward_parts(7, 8)
    rs_a1.begin(7)
    forward_parts(5, 6)
    rs_a1.begin(5)
    forward_parts(3, 4)
    rs_a1.begin(3)
    forward_parts(2, 3)
    rs_a1.begin(2)
    pull_mixed(g1, 4, 6)
    pull_mixed(g1, 7, 8)
    backward_attention(1)
    backward_parts(4, 5)
    rs_g1.begin(4)
    backward_parts(7, 8)
    rs_g1.begin(7)
    forward_parts(6, 7)
    rs_a1.last(0)
    backward_parts(5, 6)
    rs_g1.begin(5)
    forward_parts(0, 1)
    send_totals(1)
    rs_a1.last(1)
    backward_parts(2, 3)
    rs_g1.begin(2)
    backward_parts(0, 1)
    backward_parts(6, 7)
    backward_parts(1, 2)
    forward_parts(1, 2)
    rs_a1.across(1)
    rs_a1.across(0)
    rs_g1.last(0)
    backward_parts(3, 4)
    rs_g1.begin(3)
    rs_g1.last(1)
    rs_a1.along_up()
    rs_a1.along_down()
    rs_g1.across(0)
    rs_g1.across(1)
    rs_g1.along_down()
    rs_g1.along_up()
    act_finish(1, a1, rs_a1, 0)
    act_finish(1, a1, rs_a1, 1)
    grad_finish(1, g1, s1, rs_g1, 0)
    grad_finish(1, g1, s1, rs_g1, 1)

    for one in (a0, g0, s0, s1, a1, g1, rs_a0, rs_g0, rs_a1, rs_g1):
        one.drain()
    for tick in range(2):
        rest = totals.at[tick, pl.ds(1, 7)]
        pltpu.make_async_copy(rest, rest, tot_sent.at[tick]).wait()
    for one in recalls:
        one.wait_send()
    for i in range(2):
        shift(0, i, 1).wait_send()
        shift(1, i, -1).wait_send()


def per_device(
    act_in, grad_in, held_stash, new_batch, head_grad, norm_gain, w_query, w_key, w_value, w_out
):
    rows, width = act_in.shape[1:]
    half = rows // 2
    q_cols, k_cols = w_query.shape[2], w_key.shape[2]
    cols = q_cols + 2 * k_cols
    vmem = pl.BlockSpec(memory_space=pltpu.VMEM)
    hbm = pl.BlockSpec(memory_space=pl.ANY)
    out = pltpu.VMEM((2, 2, half, width), BF16)
    scratch = [
        pltpu.VMEM((8, width, cols), BF16),
        pltpu.VMEM((8, q_cols, width), BF16),
        pltpu.VMEM((8, 1, width), F32),
        pltpu.VMEM((2, rows, width), BF16),
        pltpu.VMEM((6, 8, 2, half, width), BF16),
        pltpu.VMEM((8, rows, width), F32),
        pltpu.VMEM((8, rows, width), F32),
        pltpu.VMEM((4, 8, 2, half, width), BF16),
        pltpu.VMEM((4, 8, 2, half, width), BF16),
        pltpu.VMEM((rows, cols), F32),
        pltpu.VMEM((2, rows, cols), F32),
        pltpu.VMEM((rows, q_cols), F32),
        pltpu.VMEM((rows, HD), F32),
        pltpu.VMEM((2, rows, HD), F32),
        pltpu.VMEM((rows, q_cols), BF16),
        pltpu.VMEM((rows, cols), BF16),
        pltpu.VMEM((2, 2, half, width), BF16),
        pltpu.VMEM((2, 8, 8, rows), F32),
        pltpu.VMEM((2, 8, rows), F32),
        pltpu.SemaphoreType.DMA((6, 8, 2)),
        pltpu.SemaphoreType.DMA((6,)),
        pltpu.SemaphoreType.DMA((4, 8, 2)),
        pltpu.SemaphoreType.DMA((4,)),
        pltpu.SemaphoreType.DMA((2, 8)),
        pltpu.SemaphoreType.DMA((2,)),
        pltpu.SemaphoreType.DMA((2,)),
        pltpu.SemaphoreType.DMA((2,)),
        pltpu.SemaphoreType.DMA((2, 2)),
        pltpu.SemaphoreType.DMA((2, 2)),
        pltpu.SemaphoreType.DMA((5,)),
        pltpu.SemaphoreType.DMA((2,)),
    ]
    acts, grads = pl.pallas_call(
        kernel,
        out_shape=(out, out),
        in_specs=[hbm] * 10,
        out_specs=(vmem, vmem),
        scratch_shapes=scratch,
        compiler_params=pltpu.CompilerParams(
            collective_id=0, has_side_effects=True, vmem_limit_bytes=60 << 20
        ),
    )(
        act_in.reshape(2, half, width),
        grad_in.reshape(2, half, width),
        held_stash.reshape(2, 2, half, width),
        new_batch,
        head_grad,
        norm_gain.reshape(8, 1, width),
        w_query.reshape(8, width, q_cols),
        w_key.reshape(8, width, k_cols),
        w_value.reshape(8, width, k_cols),
        w_out[0],
    )
    shape = (1, 2, rows, width)
    return acts.reshape(shape), grads.reshape(shape)


def solution(mesh):
    in_specs = (
        P("section", None, "tensor"),
        P("section", None, "tensor"),
        P("section", None, None, "tensor"),
        P(None, "tensor"),
        P(None, "tensor"),
        P("section", None),
        P("section", None, "tensor"),
        P("section", None, "tensor"),
        P("section", None, "tensor"),
        P("section", "tensor", None),
    )
    out_specs = (P("section", None, None, "tensor"), P("section", None, None, "tensor"))
    return jax.shard_map(
        per_device, mesh=mesh, in_specs=in_specs, out_specs=out_specs, check_vma=False
    )
```

```python
import functools

import jax
import jax.numpy as jnp
from jax import lax
from jax.experimental import pallas as pl
from jax.experimental.pallas import tpu as pltpu
from jax.sharding import PartitionSpec as P

HD = 128
EPS = 1e-05
MESH = pl.DeviceIdType.MESH
F32 = jnp.float32
BF16 = jnp.bfloat16

STRIP = 16
REL = [(0, 0), (0, 1), (1, 0), (3, 0), (1, 1), (3, 1), (2, 0), (2, 1)]


def split_bf16(a):
    hi = a.astype(BF16)
    return hi, (a - hi.astype(F32)).astype(BF16)


def mm3(a, b, dims):
    a_hi, a_lo = split_bf16(a)
    b_hi, b_lo = split_bf16(b)

    def dot(u, w):
        return lax.dot_general(u, w, (dims, ((), ())), preferred_element_type=F32)

    return dot(a_hi, b_hi) + (dot(a_hi, b_lo) + dot(a_lo, b_hi))


NN = ((1,), (0,))
NT = ((1,), (1,))


def heads_to_rows(a):
    return jnp.concatenate([a[:, i : i + HD] for i in range(0, a.shape[1], HD)], axis=0)


def rows_to_heads(a, rows):
    return jnp.concatenate([a[i : i + rows] for i in range(0, a.shape[0], rows)], axis=1)


def softmax_probs(query_rows, keys, rows):
    scores = mm3(query_rows, keys, NT) * HD ** (-0.5)
    row = lax.broadcasted_iota(jnp.int32, (rows, rows), 0)
    col = lax.broadcasted_iota(jnp.int32, (rows, rows), 1)
    causal = jnp.concatenate([row >= col] * (scores.shape[0] // rows), axis=0)
    scores = jnp.where(causal, scores, -1e30)
    expo = jnp.exp(scores - jnp.max(scores, axis=-1, keepdims=True))
    return expo / jnp.sum(expo, axis=-1, keepdims=True)


class Gather:
    strips = {(5, 0): (3, 0), (4, 1): (2, 1)}

    def __init__(self, buf, recv, sent, dev, source, flip):
        self.buf, self.recv, self.sent, self.dev = buf, recv, sent, dev
        self.source, self.flip = source, flip
        self.here = set()

    def copy(self, src, dst, half, to):
        rows = self.buf.shape[2]
        lo = STRIP if (dst, half) in self.strips else 0
        at = pl.ds(lo, rows - lo)
        return pltpu.make_async_remote_copy(
            src_ref=self.buf.at[src, half, at],
            dst_ref=self.buf.at[dst, half, at],
            send_sem=self.sent,
            recv_sem=self.recv.at[dst, half],
            device_id=self.dev(*to),
            device_id_type=MESH,
        )

    def strip(self, dst, half):
        at = pl.ds(0, STRIP)
        src, _ = self.strips[dst, half]
        return pltpu.make_async_remote_copy(
            src_ref=self.buf.at[src, half, at],
            dst_ref=self.buf.at[dst, half, at],
            send_sem=self.sent,
            recv_sem=self.recv.at[0, half],
            device_id=self.dev(0, 1),
            device_id_type=MESH,
        )

    def ready(self, slot, halves=(0, 1)):
        for half in halves:
            if slot and (slot, half) not in self.here:
                self.here.add((slot, half))
                self.copy(slot, slot, half, (0, 1)).wait_recv()
                if (slot, half) in self.strips:
                    self.strip(slot, half).wait_recv()

    def start(self, half):
        self.source(self, half)
        self.copy(0, 1, half, (0, 1)).start()
        self.copy(0, 3, half, (1, 0)).start()
        self.copy(0, 2, 1 - half if self.flip else half, (3, 0)).start()

    def across(self, half):
        self.ready(1, (half,))
        self.copy(1, 5, half, (1, 0)).start()
        self.copy(1, 4, half, (3, 0)).start()

    def along_up(self):
        self.ready(3, (0,))
        self.copy(3, 6, 0, (1, 0)).start()
        self.strip(5, 0).start()

    def along_down(self):
        self.ready(2, (1,))
        self.copy(2, 6, 1, (3, 0)).start()
        self.strip(4, 1).start()

    def last(self, half):
        self.ready(6, (half,))
        self.copy(6, 7, half, (0, 1)).start()

    def drain(self):
        rest = self.buf.at[pl.ds(1, 7)]
        pltpu.make_async_copy(rest, rest, self.sent).wait()


class Scatter:
    def __init__(self, parts, out, got, recv, sent, dev):
        self.parts, self.out, self.got = parts, out, got
        self.recv, self.sent, self.dev = recv, sent, dev
        self.half_rows = out.shape[2]

    def copy(self, slot, half, to, lo=0, hi=None, recv=None):
        at = pl.ds(lo, (hi or self.half_rows) - lo)
        return pltpu.make_async_remote_copy(
            src_ref=self.out.at[slot, half, at],
            dst_ref=self.got.at[slot, half, at],
            send_sem=self.sent,
            recv_sem=self.recv.at[slot if recv is None else recv, half],
            device_id=self.dev(*to),
            device_id_type=MESH,
        )

    def body(self, slot, half, to):
        return self.copy(slot, half, to, STRIP if (slot, half) in Gather.strips else 0)

    def strip(self, slot, half):
        return self.copy(slot, half, (0, 1), 0, STRIP, recv=0)

    def wait(self, slot, half):
        self.body(slot, half, (0, 1)).wait_recv()

    def part(self, slot, half):
        return self.parts[slot, pl.ds(half * self.half_rows, self.half_rows), :]

    def block(self, slot, half, strip):
        if strip is None:
            return self.got[slot, half].astype(F32)
        lo, hi = (0, STRIP) if strip else (STRIP, self.half_rows)
        piece = self.got[slot, half, lo:hi].astype(F32)
        blank = jnp.zeros((self.half_rows - (hi - lo), piece.shape[1]), F32)
        return jnp.concatenate([piece, blank] if strip else [blank, piece], axis=0)

    def push(self, slot, half, to, adds=()):
        total = self.part(slot, half)
        for other, strip in adds:
            total = total + self.block(other, half, strip)
        self.out[slot, half] = total.astype(BF16)
        self.body(slot, half, to).start()
        if (slot, half) in Gather.strips:
            self.strip(slot, half).start()

    def begin(self, slot):
        to = {7: (0, 1), 4: (1, 0), 5: (3, 0), 2: (1, 0), 3: (3, 0)}[slot]
        for half in {2: (0,), 3: (1,)}.get(slot, (0, 1)):
            self.push(slot, half, to)

    def last(self, half):
        self.wait(7, half)
        self.push(6, half, (1, 0) if half else (3, 0), [(7, None)])

    def across(self, half):
        self.wait(4, half)
        self.wait(5, half)
        self.push(1, half, (0, 1), [(4, False if half else None), (5, None if half else False)])

    def along_down(self):
        self.wait(6, 0)
        self.strip(5, 0).wait_recv()
        self.push(3, 0, (3, 0), [(6, None), (5, True)])

    def along_up(self):
        self.wait(6, 1)
        self.strip(4, 1).wait_recv()
        self.push(2, 1, (1, 0), [(6, None), (4, True)])

    def total(self, half):
        for slot in (1, 2, 3):
            self.wait(slot, half)
        total = self.part(0, half)
        for slot in (1, 2, 3):
            total = total + self.got[slot, half].astype(F32)
        return total

    def drain(self):
        rest = self.out.at[pl.ds(1, 7)]
        pltpu.make_async_copy(rest, rest, self.sent).wait()


def kernel(
    act_ref, grad_ref, stash_ref, fresh_ref, head_ref, gain_ref, wq_ref, wk_ref, wv_ref, wo_ref,
    act_out, grad_out,
    w_in, w_out, gains, edges, ag, parts_f, parts_b, outs, gots, acc_f, acc_s, acc_d, sq_f, sq_s,
    mixed_ref, dqkv_ref, moved, totals, total_out,
    ag_recv, ag_sent, rs_recv, rs_sent, tot_recv, tot_sent, recall_send, recall_recv,
    move_send, move_recv, load_sem, w_sem,
):
    n_section = lax.axis_size("section")
    section = lax.axis_index("section")
    tensor = lax.axis_index("tensor")
    place_y, place_z = tensor // 2, lax.rem(tensor, 2)
    half, width = act_ref.shape[1:]
    rows = 2 * half
    q_cols = wq_ref.shape[2]
    k_cols = wk_ref.shape[2]
    full_width = 8 * width

    def owner(dy, dz):
        return lax.rem(place_y + dy, 4) * 2 + lax.rem(place_z + dz, 2)

    def dev(dy, dz):
        return (section, owner(dy, dz))

    def sec(by):
        return (lax.rem(section + by + n_section, n_section), tensor)

    barrier = pltpu.get_barrier_semaphore()
    for dy, dz in REL[1:]:
        pl.semaphore_signal(barrier, inc=1, device_id=dev(dy, dz), device_id_type=MESH)
    for by in (1, -1, n_section // 2):
        pl.semaphore_signal(barrier, inc=1, device_id=sec(by), device_id_type=MESH)

    def own(one, half):
        pass

    def recalled(tick):
        def source(one, half):
            if half == 0:
                recalls[tick].wait_recv()

        return source

    def arrived(index, at_edge):
        def source(one, part):
            shift(index, part, 1).wait_recv()
            edge = edges[index, pl.ds(part * half, half), :]
            one.buf[0, part] = jnp.where(at_edge, edge, moved[index, part])

        return source

    sources = (
        own, own, recalled(0), recalled(1),
        arrived(0, section == 0), arrived(1, section == n_section - 1),
    )
    a0, g0, s0, s1, a1, g1 = [
        Gather(ag.at[i], ag_recv.at[i], ag_sent.at[i], dev, source, i < 4)
        for i, source in enumerate(sources)
    ]
    rs_a0, rs_g0, rs_a1, rs_g1 = [
        Scatter(parts, outs.at[i], gots.at[i], rs_recv.at[i], rs_sent.at[i], dev)
        for i, parts in enumerate((parts_f, parts_b, parts_f, parts_b))
    ]

    loads = [
        pltpu.make_async_copy(act_ref, a0.buf.at[0], load_sem.at[0]),
        pltpu.make_async_copy(grad_ref, g0.buf.at[0], load_sem.at[1]),
    ]
    for slot, (dy, dz) in enumerate(REL):
        loads.append(pltpu.make_async_copy(gain_ref.at[owner(dy, dz)], gains.at[slot], load_sem.at[2]))
    for slot, (dy, dz) in enumerate(REL):
        who = owner(dy, dz)
        loads += [
            pltpu.make_async_copy(wq_ref.at[who], w_in.at[slot, :, pl.ds(0, q_cols)], w_sem.at[0]),
            pltpu.make_async_copy(wk_ref.at[who], w_in.at[slot, :, pl.ds(q_cols, k_cols)], w_sem.at[0]),
            pltpu.make_async_copy(wv_ref.at[who], w_in.at[slot, :, pl.ds(q_cols + k_cols, k_cols)], w_sem.at[0]),
        ]
    for slot, (dy, dz) in enumerate(REL):
        at = pl.ds(pl.multiple_of(owner(dy, dz) * width, width), width)
        loads.append(pltpu.make_async_copy(wo_ref.at[:, at], w_out.at[slot], w_sem.at[1]))
    loads += [
        pltpu.make_async_copy(fresh_ref, edges.at[0], load_sem.at[3]),
        pltpu.make_async_copy(head_ref, edges.at[1], load_sem.at[4]),
    ]
    for load in loads[:10]:
        load.start()
    loads[0].wait()
    loads[1].wait()
    pl.semaphore_wait(barrier, 10)

    recalls = [
        pltpu.make_async_remote_copy(
            src_ref=stash_ref.at[tick],
            dst_ref=one.buf.at[0],
            send_sem=recall_send.at[tick],
            recv_sem=recall_recv.at[tick],
            device_id=sec(n_section // 2),
            device_id_type=MESH,
        )
        for tick, one in enumerate((s0, s1))
    ]

    def shift(index, part, by):
        return pltpu.make_async_remote_copy(
            src_ref=(act_out, grad_out)[index].at[0, part],
            dst_ref=moved.at[index, part],
            send_sem=move_send.at[index, part],
            recv_sem=move_recv.at[index, part],
            device_id=sec(by),
            device_id_type=MESH,
        )

    def clear(*refs):
        for ref in refs:
            ref[...] = jnp.zeros_like(ref)

    def whole(buf, slot):
        return buf[slot].reshape(rows, width)

    def project(one, acc, squares, lo, hi):
        for slot in range(lo, hi):
            one.ready(slot)

        @pl.loop(lo, hi)
        def _(slot):
            x = whole(one.buf, slot).astype(F32)
            square = x * x
            squares[...] += sum(square[:, i : i + HD] for i in range(0, width, HD))
            scaled = (x * gains[slot]).astype(BF16)
            acc[...] += jnp.dot(scaled, w_in[slot], preferred_element_type=F32)

    def pull_mixed(one, lo, hi):
        for slot in range(lo, hi):
            one.ready(slot)

        @pl.loop(lo, hi)
        def _(slot):
            acc_d[...] += lax.dot_general(
                whole(one.buf, slot), w_out[slot], (NT, ((), ())), preferred_element_type=F32
            )

    def inverse_rms(squares):
        mean = jnp.sum(squares, axis=-1, keepdims=True) / full_width
        return lax.rsqrt(mean + EPS)

    def forward_attention():
        qkv = acc_f[...] * inverse_rms(sq_f[...])
        query = heads_to_rows(qkv[:, :q_cols])
        keys = qkv[:, q_cols : q_cols + k_cols]
        values = qkv[:, q_cols + k_cols :]
        probs = softmax_probs(query, keys, rows)
        mixed_ref[...] = rows_to_heads(mm3(probs, values, NN), rows).astype(BF16)

    def forward_parts(lo, hi):
        @pl.loop(lo, hi)
        def _(slot):
            parts_f[slot] = jnp.dot(mixed_ref[...], w_out[slot], preferred_element_type=F32)

    def backward_parts(lo, hi):
        @pl.loop(lo, hi)
        def _(slot):
            parts_b[slot] = lax.dot_general(
                dqkv_ref[...], w_in[slot], (NT, ((), ())), preferred_element_type=F32
            )

    def diagonal():
        row = lax.broadcasted_iota(jnp.int32, (rows, rows), 0)
        col = lax.broadcasted_iota(jnp.int32, (rows, rows), 1)
        return row == col

    def total_copy(tick, mirror, dy, dz):
        return pltpu.make_async_remote_copy(
            src_ref=total_out.at[tick],
            dst_ref=totals.at[tick, mirror],
            send_sem=tot_sent.at[tick],
            recv_sem=tot_recv.at[tick, mirror],
            device_id=dev(dy, dz),
            device_id_type=MESH,
        )

    def backward_attention(tick):
        raw = acc_s[tick]
        qkv = raw * inverse_rms(sq_s[tick])
        query = heads_to_rows(qkv[:, :q_cols])
        keys = qkv[:, q_cols : q_cols + k_cols]
        values = qkv[:, q_cols + k_cols :]
        probs = softmax_probs(query, keys, rows)
        d_mixed = heads_to_rows(acc_d[...])
        d_values = mm3(probs.T, d_mixed, NN)
        d_probs = mm3(d_mixed, values, NT)
        d_scores = probs * (d_probs - jnp.sum(d_probs * probs, axis=-1, keepdims=True))
        d_scores = d_scores * HD ** (-0.5)
        d_query = rows_to_heads(mm3(d_scores, keys, NN), rows)
        d_keys = mm3(d_scores.T, query, NN)
        dqkv = jnp.concatenate([d_query, d_keys, d_values], axis=1).astype(BF16)
        dqkv_ref[...] = dqkv
        share = jnp.sum(dqkv.astype(F32) * raw, axis=-1, keepdims=True)
        line = jnp.sum(jnp.where(diagonal(), share, 0.0), axis=0, keepdims=True)
        total_out[tick] = jnp.broadcast_to(line, total_out.shape[1:])

    def send_totals(tick):
        for dy, dz in REL[1:]:
            total_copy(tick, REL.index(((4 - dy) % 4, dz)), dy, dz).start()

    def act_finish(tick, one, rs, i):
        out = (one.buf[0, i].astype(F32) + rs.total(i)).astype(BF16)
        act_out[tick, i] = out
        if tick == 0:
            shift(0, i, 1).start()

    def grad_finish(tick, one, stashed, rs, i):
        if i == 0:
            for slot in range(1, 8):
                total_copy(tick, slot, 0, 1).wait_recv()
        line = total_out[tick]
        for slot in range(1, 8):
            line = line + totals[tick, slot]
        full = jnp.where(diagonal(), line[0:1, :], 0.0)
        cut = slice(i * half, (i + 1) * half)
        row_total = jnp.sum(full[cut], axis=-1, keepdims=True)
        inv = inverse_rms(sq_s[tick, pl.ds(i * half, half), :])
        x = stashed.buf[0, i].astype(F32)
        scaled = rs.total(i) * gains[0]
        out = (
            one.buf[0, i].astype(F32)
            + inv * scaled
            - x * (inv * inv * inv) * row_total / full_width
        ).astype(BF16)
        grad_out[tick, i] = out
        if tick == 0:
            shift(1, i, -1).start()

    def start_loads():
        recalls[0].start()
        recalls[1].start()
        for load in loads[10:]:
            load.start()

    def wait_weights():
        for buf, sem in ((gains, load_sem.at[2]), (w_in, w_sem.at[0]), (w_out, w_sem.at[1])):
            pltpu.make_async_copy(buf, buf, sem).wait()
        loads[-2].wait()
        loads[-1].wait()

    a0.start(0)
    a0.start(1)
    start_loads()
    g0.start(0)
    g0.start(1)
    s0.start(0)
    a0.along_up()
    a0.along_down()
    g0.along_down()
    clear(acc_f, acc_s, acc_d, sq_f, sq_s)
    wait_weights()
    s0.start(1)
    s0.along_down()
    s0.along_up()
    g0.along_up()
    a0.last(1)
    project(s0, acc_s.at[0], sq_s.at[0], 0, 1)
    pull_mixed(g0, 0, 1)
    pull_mixed(g0, 3, 4)
    a0.across(0)
    a0.across(1)
    a0.last(0)
    g0.last(1)
    g0.last(0)
    s0.across(0)
    s0.across(1)
    project(a0, acc_f, sq_f, 0, 1)
    s0.last(0)
    project(a0, acc_f, sq_f, 2, 3)
    g0.across(0)
    s0.last(1)
    pull_mixed(g0, 2, 3)
    project(s0, acc_s.at[0], sq_s.at[0], 3, 4)
    pull_mixed(g0, 6, 7)
    g0.across(1)
    project(s0, acc_s.at[0], sq_s.at[0], 2, 3)
    pull_mixed(g0, 1, 2)
    project(a0, acc_f, sq_f, 6, 8)
    project(a0, acc_f, sq_f, 1, 2)
    project(a0, acc_f, sq_f, 3, 6)
    forward_attention()
    forward_parts(5, 8)
    rs_a0.begin(7)
    rs_a0.begin(5)
    forward_parts(4, 5)
    rs_a0.begin(4)
    project(s0, acc_s.at[0], sq_s.at[0], 4, 5)
    forward_parts(0, 1)
    project(s0, acc_s.at[0], sq_s.at[0], 1, 2)
    forward_parts(2, 3)
    pull_mixed(g0, 7, 8)
    forward_parts(3, 4)
    s1.start(0)
    s1.start(1)
    project(s1, acc_s.at[1], sq_s.at[1], 0, 1)
    pull_mixed(g0, 4, 6)
    project(s0, acc_s.at[0], sq_s.at[0], 5, 7)
    project(s0, acc_s.at[0], sq_s.at[0], 7, 8)
    backward_attention(0)
    rs_a0.last(0)
    rs_a0.last(1)
    backward_parts(0, 1)
    rs_a0.begin(2)
    backward_parts(4, 5)
    rs_g0.begin(4)
    rs_a0.begin(3)
    backward_parts(6, 8)
    rs_g0.begin(7)
    backward_parts(5, 6)
    send_totals(0)
    rs_g0.begin(5)
    rs_a0.along_up()
    forward_parts(1, 2)
    rs_a0.across(1)
    rs_g0.last(0)
    rs_a0.across(0)
    backward_parts(2, 3)
    rs_g0.last(1)
    s1.along_up()
    rs_a0.along_down()
    backward_parts(1, 2)
    rs_g0.across(0)
    rs_g0.across(1)
    backward_parts(3, 4)
    rs_g0.begin(3)
    rs_g0.along_down()
    s1.along_down()
    rs_g0.begin(2)
    rs_g0.along_up()
    s1.across(0)
    act_finish(0, a0, rs_a0, 0)
    s1.across(1)
    act_finish(0, a0, rs_a0, 1)
    s1.last(0)
    clear(acc_f, sq_f)
    grad_finish(0, g0, s0, rs_g0, 0)
    grad_finish(0, g0, s0, rs_g0, 1)
    a1.start(0)
    a1.start(1)
    g1.start(0)
    a1.along_up()
    s1.last(1)
    clear(acc_d)
    g1.start(1)
    project(a1, acc_f, sq_f, 0, 1)
    project(s1, acc_s.at[1], sq_s.at[1], 1, 2)
    project(a1, acc_f, sq_f, 3, 4)
    a1.along_down()
    project(a1, acc_f, sq_f, 1, 2)
    project(s1, acc_s.at[1], sq_s.at[1], 5, 6)
    g1.along_up()
    a1.across(0)
    a1.last(0)
    g1.along_down()
    a1.across(1)
    a1.last(1)
    g1.across(0)
    project(a1, acc_f, sq_f, 6, 7)
    g1.across(1)
    project(a1, acc_f, sq_f, 2, 3)
    pull_mixed(g1, 0, 3)
    project(s1, acc_s.at[1], sq_s.at[1], 6, 7)
    g1.last(0)
    pull_mixed(g1, 3, 4)
    project(s1, acc_s.at[1], sq_s.at[1], 2, 3)
    project(s1, acc_s.at[1], sq_s.at[1], 4, 5)
    pull_mixed(g1, 6, 7)
    project(s1, acc_s.at[1], sq_s.at[1], 7, 8)
    g1.last(1)
    project(s1, acc_s.at[1], sq_s.at[1], 3, 4)
    project(a1, acc_f, sq_f, 4, 6)
    project(a1, acc_f, sq_f, 7, 8)
    forward_attention()
    forward_parts(4, 5)
    rs_a1.begin(4)
    forward_parts(5, 6)
    rs_a1.begin(5)
    forward_parts(7, 8)
    rs_a1.begin(7)
    forward_parts(2, 3)
    rs_a1.begin(2)
    forward_parts(3, 4)
    rs_a1.begin(3)
    pull_mixed(g1, 4, 6)
    pull_mixed(g1, 7, 8)
    backward_attention(1)
    backward_parts(7, 8)
    rs_g1.begin(7)
    backward_parts(4, 5)
    rs_g1.begin(4)
    backward_parts(5, 6)
    rs_g1.begin(5)
    forward_parts(6, 7)
    forward_parts(1, 2)
    rs_a1.across(1)
    rs_a1.across(0)
    rs_a1.last(1)
    rs_a1.last(0)
    backward_parts(2, 3)
    rs_g1.begin(2)
    backward_parts(3, 4)
    backward_parts(6, 7)
    rs_g1.last(0)
    rs_g1.last(1)
    rs_g1.begin(3)
    backward_parts(1, 2)
    send_totals(1)
    forward_parts(0, 1)
    rs_a1.along_down()
    rs_a1.along_up()
    rs_g1.across(1)
    backward_parts(0, 1)
    rs_g1.along_down()
    rs_g1.across(0)
    rs_g1.along_up()
    act_finish(1, a1, rs_a1, 0)
    grad_finish(1, g1, s1, rs_g1, 0)
    act_finish(1, a1, rs_a1, 1)
    grad_finish(1, g1, s1, rs_g1, 1)

    for one in (a0, g0, s0, s1, a1, g1, rs_a0, rs_g0, rs_a1, rs_g1):
        one.drain()
    for tick in range(2):
        rest = totals.at[tick, pl.ds(1, 7)]
        pltpu.make_async_copy(rest, rest, tot_sent.at[tick]).wait()
    for one in recalls:
        one.wait_send()
    for i in range(2):
        shift(0, i, 1).wait_send()
        shift(1, i, -1).wait_send()


def per_device(
    act_in, grad_in, held_stash, new_batch, head_grad, norm_gain, w_query, w_key, w_value, w_out
):
    rows, width = act_in.shape[1:]
    half = rows // 2
    q_cols, k_cols = w_query.shape[2], w_key.shape[2]
    cols = q_cols + 2 * k_cols
    vmem = pl.BlockSpec(memory_space=pltpu.VMEM)
    hbm = pl.BlockSpec(memory_space=pl.ANY)
    out = pltpu.VMEM((2, 2, half, width), BF16)
    scratch = [
        pltpu.VMEM((8, width, cols), BF16),
        pltpu.VMEM((8, q_cols, width), BF16),
        pltpu.VMEM((8, 1, width), F32),
        pltpu.VMEM((2, rows, width), BF16),
        pltpu.VMEM((6, 8, 2, half, width), BF16),
        pltpu.VMEM((8, rows, width), F32),
        pltpu.VMEM((8, rows, width), F32),
        pltpu.VMEM((4, 8, 2, half, width), BF16),
        pltpu.VMEM((4, 8, 2, half, width), BF16),
        pltpu.VMEM((rows, cols), F32),
        pltpu.VMEM((2, rows, cols), F32),
        pltpu.VMEM((rows, q_cols), F32),
        pltpu.VMEM((rows, HD), F32),
        pltpu.VMEM((2, rows, HD), F32),
        pltpu.VMEM((rows, q_cols), BF16),
        pltpu.VMEM((rows, cols), BF16),
        pltpu.VMEM((2, 2, half, width), BF16),
        pltpu.VMEM((2, 8, 8, rows), F32),
        pltpu.VMEM((2, 8, rows), F32),
        pltpu.SemaphoreType.DMA((6, 8, 2)),
        pltpu.SemaphoreType.DMA((6,)),
        pltpu.SemaphoreType.DMA((4, 8, 2)),
        pltpu.SemaphoreType.DMA((4,)),
        pltpu.SemaphoreType.DMA((2, 8)),
        pltpu.SemaphoreType.DMA((2,)),
        pltpu.SemaphoreType.DMA((2,)),
        pltpu.SemaphoreType.DMA((2,)),
        pltpu.SemaphoreType.DMA((2, 2)),
        pltpu.SemaphoreType.DMA((2, 2)),
        pltpu.SemaphoreType.DMA((5,)),
        pltpu.SemaphoreType.DMA((2,)),
    ]
    acts, grads = pl.pallas_call(
        kernel,
        out_shape=(out, out),
        in_specs=[hbm] * 10,
        out_specs=(vmem, vmem),
        scratch_shapes=scratch,
        compiler_params=pltpu.CompilerParams(
            collective_id=0, has_side_effects=True, vmem_limit_bytes=60 << 20
        ),
    )(
        act_in.reshape(2, half, width),
        grad_in.reshape(2, half, width),
        held_stash.reshape(2, 2, half, width),
        new_batch,
        head_grad,
        norm_gain.reshape(8, 1, width),
        w_query.reshape(8, width, q_cols),
        w_key.reshape(8, width, k_cols),
        w_value.reshape(8, width, k_cols),
        w_out[0],
    )
    shape = (1, 2, rows, width)
    return acts.reshape(shape), grads.reshape(shape)


def solution(mesh):
    in_specs = (
        P("section", None, "tensor"),
        P("section", None, "tensor"),
        P("section", None, None, "tensor"),
        P(None, "tensor"),
        P(None, "tensor"),
        P("section", None),
        P("section", None, "tensor"),
        P("section", None, "tensor"),
        P("section", None, "tensor"),
        P("section", "tensor", None),
    )
    out_specs = (P("section", None, None, "tensor"), P("section", None, None, "tensor"))
    return jax.shard_map(
        per_device, mesh=mesh, in_specs=in_specs, out_specs=out_specs, check_vma=False
    )
```
